128 devices in a mesh: gx: 4 (over y), gy: 32 (over x, z, core).
Axes of the slice: x: 4, y: 4, z: 4, core: 2. Of those that a mesh axis runs over, the one named last changes fastest.
Arguments:
- blocks: float32 [4096, 8, 128, 128], P(('gx', 'gy')), may hold values from -0.1875 to 0.1875
- columns: int32 [4096, 8], P(('gx', 'gy')), may hold values from 0 to 4095, as said below
- counts: int32 [4096], P(('gx', 'gy')), may hold values from 2 to 8, as said below
- start_vectors: float32 [524288, 256], P(('gx', 'gy')), may hold values from -6 to 6
Outputs:
- basis: float32 [524288, 256], P(('gx', 'gy'))
- factor: float32 [256, 256], replicated
The draws below stay inside these ranges and needn't reach their ends.
Inputs may be any that keep to these rules, and one draw needn't show every extreme that they name: `columns`: slots below a row's count name distinct block rows within 4 of the row, slot 0 the row itself; slots at or past the count hold the row's own index. `counts`: some block row has exactly 8 live slots.
All inputs are finite; a program needn't handle non-finite values.
Results may differ from the reference program's by a relative error of at most 0.0003.
Values sent between devices are 32-bit elements; how exact they have to be, the bound alone decides.
No kernel may reach another device: no remote copies, remote signals or barrier semaphores. Data moves between devices by JAX's collectives and lax.ppermute only.
A program may use at most 192 MiB of HBM per device.

```python
import jax
import jax.numpy as jnp
from jax import lax

B = 128
K = 256
RB_DEV = 32
MAXNB = 8
REACH = 4
DEGREE = 3
NB = 4096
NROWS = 524288


def pattern_helper(key):
    key_score, key_device, key_count, key_forced = jax.random.split(key, 4)
    offsets = jnp.arange(-REACH, REACH + 1, dtype=jnp.int32)
    width_all = 2 * REACH + 1
    row_ids = jnp.arange(NB, dtype=jnp.int32)[:, None]
    targets = row_ids + offsets[None, :]
    valid = (targets >= 0) & (targets < NB)
    scores = jax.random.randint(key_score, (NB, width_all), 0, 1 << 20) * width_all + jnp.arange(width_all, dtype=jnp.int32)[None, :]
    scores = jnp.where(offsets[None, :] == 0, 1 << 30, jnp.where(valid, scores, -1))
    _, order = lax.top_k(scores, MAXNB)
    chosen = jnp.take_along_axis(targets, order, axis=1)
    valid_count = jnp.sum(valid.astype(jnp.int32), axis=1)
    device_cap = jax.random.randint(key_device, (NB // RB_DEV,), 3, MAXNB + 1)
    row_cap = jnp.repeat(device_cap, RB_DEV)
    live = jax.random.randint(key_count, (NB,), 2, row_cap + 1)
    forced_row = jax.random.randint(key_forced, (), REACH, NB - REACH)
    live = jnp.where(jnp.arange(NB, dtype=jnp.int32) == forced_row, MAXNB, live)
    live = jnp.minimum(live, valid_count)
    slot_ids = jnp.arange(MAXNB, dtype=jnp.int32)[None, :]
    chosen = jnp.where(slot_ids < live[:, None], chosen, row_ids)
    return (chosen.astype(jnp.int32), live.astype(jnp.int32))


def draw_columns(key, part):
    chosen, live = pattern_helper(key)
    return chosen


def draw_counts(key, part):
    chosen, live = pattern_helper(key)
    return live


def block_scale(rng, shape, shards, least, high):
    def one(axis_at, parts):
        heights = jax.random.uniform(jax.random.fold_in(jax.random.fold_in(rng, 6), axis_at), (parts,), jnp.float32, least / len(shards), high / len(shards))
        return jnp.repeat(jnp.exp(heights), shape[axis_at] // parts).reshape((-1,) + (1,) * (len(shape) - axis_at - 1))

    factor_of = one(*shards[0])
    for cut in shards[1:]:
        factor_of = factor_of * one(*cut)
    return factor_of


def noise(rng, dims, scale, limit, shards=(), kind=jnp.bfloat16):
    loudness = block_scale(rng, dims, shards, -0.22, 0.18) if shards else 1.0
    drawn = jax.random.normal(rng, dims, jnp.float32) * scale * loudness
    return jnp.minimum(jnp.maximum(drawn, -limit), limit).astype(kind)


def setup_inputs(seed: int = 0) -> dict:
    streams_of = jax.random.split(jax.random.key(seed), 5)
    blocks = noise(streams_of[0], (NB, MAXNB, B, B), (9 * B) ** -0.5, 0.1875, ((0, 128),), jnp.float32)
    columns = draw_columns(jax.random.fold_in(streams_of[4], 71), 0)
    counts = draw_counts(jax.random.fold_in(streams_of[4], 71), 0)
    start_vectors = noise(streams_of[3], (NROWS, K), 1.0, 6.0, ((0, 128),), jnp.float32)
    return {"blocks": blocks, "columns": columns, "counts": counts, "start_vectors": start_vectors}


def apply_hamiltonian(vectors, blocks, columns, counts):
    empty = jnp.zeros_like(vectors)

    def one_slot(state_pair, slot):
        forward, returned = state_pair
        target = columns[:, slot]
        live_mask = (slot < counts).astype(jnp.float32)[:, None, None]
        block = blocks[:, slot]
        forward = forward + live_mask * jnp.einsum('nab,nbk->nak', block, vectors[target], precision=lax.Precision.HIGHEST)
        moved = live_mask * jnp.einsum('nba,nbk->nak', block, vectors, precision=lax.Precision.HIGHEST)
        returned = returned.at[target].add(moved)
        return ((forward, returned), None)
    (forward, returned), _ = lax.scan(one_slot, (empty, empty), jnp.arange(MAXNB, dtype=jnp.int32))
    return 0.5 * (forward + returned)

def reference(blocks, columns, counts, start_vectors):
    prior = start_vectors.reshape(NB, B, K)
    current = apply_hamiltonian(prior, blocks, columns, counts)
    for level in range(DEGREE - 1):
        following = 2.0 * apply_hamiltonian(current, blocks, columns, counts) - prior
        prior, current = (current, following)
    filtered = current.reshape(NROWS, K)
    orthonormal, upper = jnp.linalg.qr(filtered)
    signs = jnp.sign(jnp.diagonal(upper))
    orthonormal = orthonormal * signs[None, :]
    upper = upper * signs[:, None]
    scale_root = jnp.sqrt(jnp.float32(NROWS))
    return (orthonormal * scale_root, upper / scale_root)
```

```python
import jax
import jax.numpy as jnp
from jax import lax
from jax.experimental import pallas as pl
from jax.experimental.pallas import tpu as pltpu
from jax.sharding import Mesh, PartitionSpec as P

B = 128
K = 256
ROWS = 32
SLOTS = 8
REACH = 4
PANELS = ROWS // 2
WIDE = 10 * B
EDGE = REACH * B
LOCAL = ROWS * B
EXT = LOCAL + 2 * EDGE
DEAD = ROWS * SLOTS
TABLE = (ROWS + 10) * 16
RING = 16
VRING = 6
KEPT = 4
PAIRS_PREV = [(r, o) for r in range(4) for o in range(-4, 0) if r + o < 0]
PAIRS_NEXT = [(r, o) for r in range(28, 32) for o in range(1, 5) if r + o > 31]
PACKED = 10 * B + 2 * EDGE

F32 = jnp.float32
BF16 = jnp.bfloat16
VM = pl.BlockSpec(memory_space=pltpu.VMEM)
SM = pl.BlockSpec(memory_space=pltpu.SMEM)
HB = pl.BlockSpec(memory_space=pltpu.HBM)
ALL = ("y", "x", "z", "c")


def params(mib):
    return pltpu.CompilerParams(vmem_limit_bytes=mib * 2**20)


def cost(flops, moved):
    return pl.CostEstimate(flops=int(flops), bytes_accessed=int(moved), transcendentals=0)


def dot(a, b):
    return jnp.dot(a, b, preferred_element_type=F32)


def split(x):
    high = x.astype(BF16)
    return high, (x - high.astype(F32)).astype(BF16)


def rows(start, size):
    return pl.ds(pl.multiple_of(start, size), size)


def place(r, o):
    return (r + 5) * 16 + o + 5


def fill_table(table, columns, counts, first, r):
    for s in range(SLOTS):
        offset = columns[s, r] - first - r
        table[jnp.where(s < counts[r], place(r, offset), TABLE)] = r * SLOTS + s


def clear_table(table, start, stop):
    for k in range(start, stop):
        table[k] = DEAD


def even_core(columns):
    return (columns[0, 0] // ROWS) % 2 == 0


def pack_kernel(columns, counts, blocks, vectors, swap_far, swap_near, table, zero, sems):
    first = columns[0, 0]
    zero[...] = jnp.zeros_like(zero)
    for r in (0, 1, 2, 3, 28, 29, 30, 31):
        clear_table(table, place(r, -4), place(r, 5))
        fill_table(table, columns, counts, first, r)

    def fill(to_prev, to_next):
        moves = []
        for side, (out, pairs) in enumerate(((to_prev, PAIRS_PREV), (to_next, PAIRS_NEXT))):
            start = 0 if side == 0 else LOCAL - EDGE
            for half in range(2):
                move = pltpu.make_async_copy(
                    vectors.at[pl.ds(start, EDGE), pl.ds(half * B, B)],
                    out.at[pl.ds(10 * B + half * EDGE, EDGE), :],
                    sems.at[side * 12 + 10 + half],
                )
                move.start()
                moves.append(move)
            for k, (r, o) in enumerate(pairs):
                slot = table[place(r, o)]
                target = out.at[pl.ds(k * B, B), :]
                sem = sems.at[side * 12 + k]

                @pl.when(slot < DEAD)
                def _():
                    pltpu.make_async_copy(blocks.at[slot], target, sem).start()

                @pl.when(slot >= DEAD)
                def _():
                    pltpu.make_async_copy(zero, target, sem).start()

                moves.append(pltpu.make_async_copy(zero, target, sem))
        for move in moves:
            move.wait()

    even = even_core(columns)

    @pl.when(even)
    def _():
        fill(swap_far, swap_near)

    @pl.when(jnp.logical_not(even))
    def _():
        fill(swap_near, swap_far)


def apply_panel(p, hh, hl, vh, vl):
    window = pl.ds(pl.multiple_of(p * 2 * B, 2 * B), WIDE)
    return dot(hh, vh[window, :]) + dot(hl, vh[window, :]) + dot(hh, vl[window, :])


def store_rows(p, value, uh, ul, part):
    at = rows(EDGE + p * 2 * B, 2 * B)
    uh[at, :], ul[at, :] = split(value)
    spare = jnp.where(p < 2, p, jnp.where(p >= PANELS - 2, p - PANELS + 4, 4))
    part[rows(spare * 2 * B, 2 * B), :] = value


def clear_pads(*refs):
    for ref in refs:
        ref[:EDGE, :] = jnp.zeros((EDGE, K), BF16)
        ref[EXT - EDGE :, :] = jnp.zeros((EDGE, K), BF16)


def first_kernel(
    columns, counts, blocks, vectors, hh, hl, vh, vl, uh, ul, part, table, sbuf, vbuf, ah, al, bh, bl, ssem, vsem
):
    def block_copy(r):
        return pltpu.make_async_copy(
            blocks.at[pl.ds(r * SLOTS, SLOTS)],
            sbuf.at[rows((r % RING) * SLOTS, SLOTS)],
            ssem.at[r % RING],
        )

    def vector_copy(q):
        return pltpu.make_async_copy(
            vectors.at[rows(q * 2 * B, 2 * B), :], vbuf.at[q % VRING], vsem.at[q % VRING]
        )

    def take_vectors(q):
        vector_copy(q).wait()
        at = rows(EDGE + q * 2 * B, 2 * B)
        vh[at, :], vl[at, :] = split(vbuf[q % VRING])

    for q in range(VRING):
        block_copy(2 * q).start()
        block_copy(2 * q + 1).start()
        vector_copy(q).start()
    for r in range(2 * VRING, RING):
        block_copy(r).start()
    sbuf[RING * SLOTS] = jnp.zeros((B, B), F32)
    clear_pads(vh, vl, uh, ul)
    first = columns[0, 0]

    def clear(r, _):
        for k in range(16):
            table[r * 16 + k] = DEAD
        return 0

    def fill(r, _):
        fill_table(table, columns, counts, first, r)
        return 0

    lax.fori_loop(0, ROWS + 10, clear, 0)
    lax.fori_loop(0, ROWS, fill, 0)

    def fetch(slot, inside=True):
        return sbuf[jnp.where(inside & (slot < DEAD), slot % (RING * SLOTS), RING * SLOTS)]

    def build(p, high, low):
        for h in range(2):
            i = 2 * p + h
            at = slice(h * B, h * B + B)
            for c in range(10):
                o = c - 4 - h
                cols = slice(c * B, c * B + B)
                if abs(o) > REACH:
                    parts = (jnp.zeros((B, B), BF16),) * 2
                else:
                    near = fetch(table[place(i, o)], (i + o >= 0) & (i + o < ROWS))
                    far = fetch(table[place(i + o, -o)])
                    parts = split(near + far.T)
                high[at, cols], low[at, cols] = parts
                hh[p, at, cols], hl[p, at, cols] = parts

    def ready(p):
        @pl.when(p < PANELS - 2)
        def _():
            block_copy(2 * p + 4).wait()
            block_copy(2 * p + 5).wait()
            take_vectors(p + 2)

            @pl.when(p + 2 + VRING < PANELS)
            def _():
                vector_copy(p + 2 + VRING).start()

    def refill(p):
        @pl.when((p >= 3) & (p < PANELS - 5))
        def _():
            block_copy(2 * p + 10).start()
            block_copy(2 * p + 11).start()

    for r in range(REACH):
        block_copy(r).wait()
    for q in range(2):
        take_vectors(q)
        vector_copy(q + VRING).start()
    ready(0)
    build(0, ah, al)

    def step(t, _):
        p = 2 * t
        refill(p)
        refill(p + 1)
        ready(p + 1)
        ready(p + 2)
        first_half = 0.5 * apply_panel(p, ah[...], al[...], vh, vl)
        build(p + 1, bh, bl)
        store_rows(p, first_half, uh, ul, part)
        second_half = 0.5 * apply_panel(p + 1, bh[...], bl[...], vh, vl)
        build(jnp.minimum(p + 2, PANELS - 1), ah, al)
        store_rows(p + 1, second_half, uh, ul, part)
        return 0

    lax.fori_loop(0, PANELS // 2, step, 0)


def inner_kernel(hh, hl, vh, vl, ph, pr, uh, ul, part):
    clear_pads(uh, ul)

    def step(p, _):
        at = rows(EDGE + p * 2 * B, 2 * B)
        prior = ph[at, :].astype(F32) + pr[at, :].astype(F32)
        store_rows(p, apply_panel(p, hh[p], hl[p], vh, vl) - prior, uh, ul, part)
        return 0

    lax.fori_loop(0, PANELS, step, 0, unroll=2)


def cross(xh, xl, side, halo_high, halo_low):
    return dot(xh[side], halo_high) + dot(xl[side], halo_high) + dot(xh[side], halo_low)


def write_edge(side, value, uh, ul):
    start = EDGE if side == 0 else LOCAL
    uh[start : start + EDGE, :], ul[start : start + EDGE, :] = split(value)


def first_edge_kernel(
    columns, sent_far, sent_near, got_far, got_near, part, uh_in, ul_in, *rest
):
    uh, ul, xh, xl, far, near, own, got, sems = rest[KEPT:]
    del uh_in, ul_in
    even = even_core(columns)

    def fetch(refs):
        moves = [
            pltpu.make_async_copy(ref, place_, sems.at[k])
            for k, (ref, place_) in enumerate(zip(refs, (own.at[0], own.at[1], got.at[0], got.at[1])))
        ]
        for move in moves:
            move.start()
        for move in moves:
            move.wait()

    @pl.when(even)
    def _():
        fetch((sent_far, sent_near, got_far, got_near))

    @pl.when(jnp.logical_not(even))
    def _():
        fetch((sent_near, sent_far, got_near, got_far))

    zero = jnp.zeros((B, B), BF16)
    for r in range(REACH):
        for c in range(REACH):
            at, cols = slice(r * B, r * B + B), slice(c * B, c * B + B)
            if c >= r:
                a = PAIRS_PREV.index((r, c - 4 - r)) * B
                b = PAIRS_NEXT.index((28 + c, 4 + r - c)) * B
                value = own[0, a : a + B, :] + got[0, b : b + B, :].T
                xh[0, at, cols], xl[0, at, cols] = split(value)
            else:
                xh[0, at, cols], xl[0, at, cols] = zero, zero
            if c <= r:
                a = PAIRS_NEXT.index((28 + r, 4 + c - r)) * B
                b = PAIRS_PREV.index((c, r - c - 4)) * B
                value = own[1, a : a + B, :] + got[1, b : b + B, :].T
                xh[1, at, cols], xl[1, at, cols] = split(value)
            else:
                xh[1, at, cols], xl[1, at, cols] = zero, zero
    values = []
    for side in range(2):
        halves = [
            split(got[side, 10 * B + half * EDGE : 10 * B + (half + 1) * EDGE, :]) for half in range(2)
        ]
        high = jnp.concatenate([halves[0][0], halves[1][0]], axis=1)
        low = jnp.concatenate([halves[0][1], halves[1][1]], axis=1)
        value = part[side * EDGE : (side + 1) * EDGE, :] + 0.5 * cross(xh, xl, side, high, low)
        write_edge(side, value, uh, ul)
        values.append(value)
    send_edges(even, values, far, near)


def send_edges(even, values, far, near):
    far[...] = jnp.where(even, values[0], values[1])
    near[...] = jnp.where(even, values[1], values[0])


def finish_edges(columns, xh, xl, got_far, got_near, part, uh, ul):
    even = even_core(columns)
    a, b = got_far[...], got_near[...]
    values = []
    for side, halo in enumerate((jnp.where(even, a, b), jnp.where(even, b, a))):
        value = part[side * EDGE : (side + 1) * EDGE, :] + cross(xh, xl, side, *split(halo))
        write_edge(side, value, uh, ul)
        values.append(value)
    return even, values


def edge_kernel(columns, xh, xl, got_far, got_near, part, uh_in, ul_in, *rest):
    uh, ul, far, near = rest[KEPT:]
    del uh_in, ul_in
    even, values = finish_edges(columns, xh, xl, got_far, got_near, part, uh, ul)
    send_edges(even, values, far, near)


def last_edge_kernel(columns, xh, xl, got_far, got_near, part, uh_in, ul_in, uh, ul, mine, theirs):
    del uh_in, ul_in
    even, _ = finish_edges(columns, xh, xl, got_far, got_near, part, uh, ul)
    over = (((0,), (0,)), ((), ()))

    def step(q, totals):
        at = rows(EDGE + q * 512, 512)
        high, low = uh[at, :], ul[at, :]
        return (
            totals[0] + lax.dot_general(high, high, over, preferred_element_type=F32),
            totals[1] + lax.dot_general(high, low, over, preferred_element_type=F32),
        )

    zero = jnp.zeros((K, K), F32)
    main, mixed = lax.fori_loop(0, LOCAL // 512, step, (zero, zero))
    total = main + mixed + mixed.T
    r = lax.broadcasted_iota(jnp.int32, (B, B), 0)
    c = lax.broadcasted_iota(jnp.int32, (B, B), 1)
    corner, beside = total[B:, B:], total[:B, B:]
    square = jnp.where(c >= r, total[:B, :B], corner)
    diagonal = jnp.broadcast_to(jnp.sum(jnp.where(r == c, corner, 0.0), axis=0, keepdims=True), (8, B))
    none = jnp.zeros((8, B), F32)
    mine[:B, :] = jnp.where(even, square, beside)
    mine[B:, :] = jnp.where(even, diagonal, none)
    theirs[:B, :] = jnp.where(even, beside, square)
    theirs[B:, :] = jnp.where(even, none, diagonal)


def precise(a, b, over=(((1,), (0,)), ((), ()))):
    return lax.dot_general(
        a, b, over, precision=lax.Precision.HIGHEST, preferred_element_type=F32
    )


def basis_kernel(columns, mine, other, uh, ul, scale, basis, factor, work, upper, inverse, out, sems):
    r = lax.broadcasted_iota(jnp.int32, (B, B), 0)
    c = lax.broadcasted_iota(jnp.int32, (B, B), 1)
    even = even_core(columns)
    ad = jnp.where(even, mine[...], other[...])
    b = jnp.where(even, other[:B, :], mine[:B, :])
    square = ad[:B, :]
    high_part = jnp.where(c >= r, square, 0.0)
    low_part = jnp.where(c < r, square, 0.0)
    work[:B, :B] = high_part + jnp.where(c > r, square, 0.0).T
    work[:B, B:] = b
    work[B:, :B] = b.T
    work[B:, B:] = low_part + low_part.T + jnp.where(r == c, ad[B : B + 1, :], 0.0)

    r = lax.broadcasted_iota(jnp.int32, (K, K), 0)
    c = lax.broadcasted_iota(jnp.int32, (K, K), 1)
    gram = work[...]
    eye = jnp.where(r == c, 1.0, 0.0).astype(F32)
    on = jnp.where(r == c, gram, 0.0)
    row_d = jnp.sum(on, axis=0, keepdims=True)
    col_d = jnp.sum(on, axis=1, keepdims=True)
    row_s, col_s = lax.rsqrt(row_d), lax.rsqrt(col_d)
    scaled = gram * row_s * col_s
    work[...] = scaled
    gap = jnp.where(r == c, 0.0, scaled)

    def half_upper(e):
        return jnp.where(c > r, e, jnp.where(c == r, 0.5 * e, 0.0))

    left = (((0,), (0,)), ((), ()))

    def more(state):
        return (state[0] > 1e-8) & (state[0] < 4.0) & (state[1] < 12)

    def newton(state):
        _, count, y = state
        e = precise(y, precise(scaled, y), left) - eye
        return (jnp.sum(e * e), count + 1, y - precise(y, half_upper(e)))

    size, _, y = lax.while_loop(more, newton, (jnp.sum(gap * gap), 0, eye - half_upper(gap)))
    settled = (size <= 1e-8) & (jnp.min(jnp.where(r == c, y, 1.0)) > 0.0)

    @pl.when(settled)
    def _():
        inverse[...] = y
        full = precise(y, scaled, left)
        upper[...] = jnp.where(c >= r, full, 0.0)

    @pl.when(jnp.logical_not(settled))
    def _():
        lane = lax.broadcasted_iota(jnp.int32, (1, K), 1)
        down = lax.broadcasted_iota(jnp.int32, (K, 1), 0)

        def column(k, _):
            a = work[...]
            row = work[pl.ds(k, 1), :]
            root = lax.rsqrt(jnp.sum(jnp.where(lane == k, row, 0.0)))
            row = jnp.where(lane >= k, row * root, 0.0)
            col = jnp.sum(jnp.where(c == k, a, 0.0), axis=1, keepdims=True)
            col = jnp.where(down >= k, col * root, 0.0)
            upper[pl.ds(k, 1), :] = row
            work[...] = a - col * row
            return 0

        lax.fori_loop(0, K, column, 0)
        inverse[...] = jnp.zeros((K, K), F32)

        def back(t, _):
            k = K - 1 - t
            row = upper[pl.ds(k, 1), :]
            pivot = jnp.sum(jnp.where(lane == k, row, 0.0))
            rest = jnp.broadcast_to(jnp.where(lane > k, row, 0.0), (8, K))
            known = precise(rest, inverse[...])[:1, :]
            inverse[pl.ds(k, 1), :] = (jnp.where(lane == k, 1.0, 0.0) - known) / pivot
            return 0

        lax.fori_loop(0, K, back, 0)

    root = scale[0]
    factor[...] = upper[...] * (row_d * row_s) / root
    wh, wl = split(inverse[...] * (col_s * root))

    def out_copy(q):
        at = rows(q * 256, 256)
        return pltpu.make_async_copy(out.at[at, :], basis.at[at, :], sems.at[q])

    def step(q, _):
        at = rows(EDGE + q * 256, 256)
        out[rows(q * 256, 256), :] = dot(uh[at, :], wh) + dot(ul[at, :], wh) + dot(uh[at, :], wl)
        out_copy(q).start()
        return 0

    lax.fori_loop(0, LOCAL // 256, step, 0, unroll=2)
    for q in range(LOCAL // 256):
        out_copy(q).wait()


def swap_pairs(far, near):
    count = lax.axis_size(ALL)
    pairs = [(i, i + 1) for i in range(1, count - 1, 2)]
    got_far = lax.ppermute(far, ALL, pairs + [(j, i) for i, j in pairs])
    got_near = lax.ppermute(near, "c", [(0, 1), (1, 0)])
    return got_far, got_near


def group_sum(value, axis):
    count = lax.axis_size(axis)
    one, two, three = (
        lax.ppermute(value, axis, [(i, i ^ k) for i in range(count)]) for k in (1, 2, 3)
    )
    return (value + one) + (two + three)


def body(blocks, columns, counts, start_vectors):
    flat, start_vectors, counts, columns = (
        pltpu.with_memory_space_constraint(x, pltpu.HBM)
        for x in (blocks.reshape(DEAD, B, B), start_vectors, counts, columns.T)
    )
    packed = pltpu.HBM((PACKED, B), F32)
    sent = pl.pallas_call(
        pack_kernel,
        out_shape=(packed, packed),
        in_specs=(SM, SM, HB, HB),
        out_specs=(HB, HB),
        scratch_shapes=[
            pltpu.SMEM((TABLE + 1,), jnp.int32),
            pltpu.VMEM((B, B), F32),
            pltpu.SemaphoreType.DMA((24,)),
        ],
        compiler_params=params(2),
        cost_estimate=cost(0, 2 * 2 * PACKED * B * 4),
        name="pack_edges",
    )(columns, counts, flat, start_vectors)
    sent = [pltpu.with_memory_space_constraint(x, pltpu.HBM) for x in sent]
    got = swap_pairs(*sent)

    wide = pltpu.VMEM((PANELS, 2 * B, WIDE), BF16)
    slab = pltpu.VMEM((EXT, K), BF16)
    partial = pltpu.VMEM((10 * B, K), F32)
    crossing = pltpu.VMEM((2, EDGE, EDGE), BF16)
    edge = jax.ShapeDtypeStruct((EDGE, K), F32)
    flops = 3 * 2 * PANELS * 2 * B * WIDE * K
    hh, hl, vh, vl, uh, ul, part = pl.pallas_call(
        first_kernel,
        out_shape=(wide, wide, slab, slab, slab, slab, partial),
        in_specs=(SM, SM, HB, HB),
        out_specs=(VM,) * 7,
        scratch_shapes=[
            pltpu.SMEM((TABLE + 1,), jnp.int32),
            pltpu.VMEM((RING * SLOTS + 1, B, B), F32),
            pltpu.VMEM((VRING, 2 * B, K), F32),
        ]
        + [pltpu.VMEM((2 * B, WIDE), BF16)] * 4
        + [pltpu.SemaphoreType.DMA((RING,)), pltpu.SemaphoreType.DMA((VRING,))],
        compiler_params=params(14),
        cost_estimate=cost(flops * 2, 24 * 2**20),
        name="first_inner",
    )(columns, counts, flat, start_vectors)

    uh, ul, xh, xl, far, near = pl.pallas_call(
        first_edge_kernel,
        out_shape=(slab, slab, crossing, crossing, edge, edge),
        in_specs=(SM,) + (HB,) * 4 + (VM,) * (3 + KEPT),
        out_specs=(VM,) * 6,
        input_output_aliases={6: 0, 7: 1},
        scratch_shapes=[pltpu.VMEM((2, PACKED, B), F32)] * 2 + [pltpu.SemaphoreType.DMA((4,))],
        compiler_params=params(8),
        cost_estimate=cost(8e8, 6 * 2**20),
        name="first_edge",
    )(columns, *sent, *got, part, uh, ul, hh, hl, vh, vl)

    def inner(vectors, prior):
        return pl.pallas_call(
            inner_kernel,
            out_shape=(slab, slab, partial),
            in_specs=(VM,) * 6,
            out_specs=(VM,) * 3,
            compiler_params=params(6),
            cost_estimate=cost(flops, 2**20),
            name="inner",
        )(hh, hl, *vectors, *prior)

    got = swap_pairs(far, near)
    wh, wl, part = inner((uh, ul), (vh, vl))
    wh, wl, far, near = pl.pallas_call(
        edge_kernel,
        out_shape=(slab, slab, edge, edge),
        in_specs=(SM,) + (VM,) * (7 + KEPT),
        out_specs=(VM,) * 4,
        input_output_aliases={6: 0, 7: 1},
        compiler_params=params(8),
        cost_estimate=cost(8e8, 2 * 2**20),
        name="edge",
    )(columns, xh, xl, *got, part, wh, wl, hh, hl, uh, ul)

    got = swap_pairs(far, near)
    fh, fl, part = inner((wh, wl), (uh, ul))
    half = pltpu.VMEM((B + 8, B), F32)
    fh, fl, mine, theirs = pl.pallas_call(
        last_edge_kernel,
        out_shape=(slab, slab, half, half),
        in_specs=(SM,) + (VM,) * 7,
        out_specs=(VM,) * 4,
        input_output_aliases={6: 0, 7: 1},
        compiler_params=params(8),
        cost_estimate=cost(2e9, 2 * 2**20),
        name="last_edge_gram",
    )(columns, xh, xl, *got, part, fh, fl)

    swap = [(0, 1), (1, 0)]
    mine = mine + lax.ppermute(theirs, "c", swap)
    for axis in ("y", "x", "z"):
        mine = group_sum(mine, axis)
    other = lax.ppermute(mine, "c", swap)

    total_rows = LOCAL * lax.axis_size(ALL)
    scale = jnp.sqrt(jnp.float32(total_rows)).reshape(1)
    basis, factor = pl.pallas_call(
        basis_kernel,
        out_shape=(jax.ShapeDtypeStruct((LOCAL, K), F32), jax.ShapeDtypeStruct((K, K), F32)),
        in_specs=(SM, VM, VM, VM, VM, SM),
        out_specs=(HB, VM),
        scratch_shapes=[pltpu.VMEM((K, K), F32)] * 3
        + [pltpu.VMEM((LOCAL, K), F32), pltpu.SemaphoreType.DMA((LOCAL // 256,))],
        compiler_params=params(10),
        cost_estimate=cost(2e9, 4 * 2**20),
        name="basis",
    )(columns, mine, other, fh, fl, scale)
    return basis, factor


def solution(mesh):
    fine = Mesh(mesh.devices.reshape(4, 4, 4, 2), ALL)
    placed = (P(ALL, None, None, None), P(ALL, None), P(ALL), P(ALL, None))
    return jax.shard_map(
        body, mesh=fine, in_specs=placed, out_specs=(P(ALL, None), P()), check_vma=False
    )
```

```python
import jax
import jax.numpy as jnp
from jax import lax
from jax.experimental import pallas as pl
from jax.experimental.pallas import tpu as pltpu
from jax.sharding import Mesh, PartitionSpec as P

B = 128
K = 256
ROWS = 32
SLOTS = 8
REACH = 4
PANELS = ROWS // 2
WIDE = 10 * B
EDGE = REACH * B
LOCAL = ROWS * B
DEAD = ROWS * SLOTS
TABLE = (ROWS + 10) * 16
RING = 24
VRING = 8
GROUPS = ((0, 1), (2, 3, 4, 5), (6, 7, 8, 9), (10, 11, 12, 13), (14, 15))
KEPT = 4
CHUNK = 1024
PAIRS_PREV = [(r, o) for r in range(4) for o in range(-4, 0) if r + o < 0]
PAIRS_NEXT = [(r, o) for r in range(28, 32) for o in range(1, 5) if r + o > 31]
PACKED = 10 * B + 2 * EDGE

F32 = jnp.float32
BF16 = jnp.bfloat16
VM = pl.BlockSpec(memory_space=pltpu.VMEM)
SM = pl.BlockSpec(memory_space=pltpu.SMEM)
HB = pl.BlockSpec(memory_space=pltpu.HBM)
ALL = ("y", "x", "z", "c")


def params(mib):
    return pltpu.CompilerParams(vmem_limit_bytes=mib * 2**20)


def cost(flops, moved):
    return pl.CostEstimate(flops=int(flops), bytes_accessed=int(moved), transcendentals=0)


def dot(a, b):
    return jnp.dot(a, b, preferred_element_type=F32)


def split(x):
    high = x.astype(BF16)
    return high, (x - high.astype(F32)).astype(BF16)


def rows(start, size):
    return pl.ds(pl.multiple_of(start, size), size)


def place(r, o):
    return (r + 5) * 16 + o + 5


def fill_table(table, columns, counts, first, r):
    for s in range(SLOTS):
        offset = columns[s, r] - first - r
        table[jnp.where(s < counts[r], place(r, offset), TABLE)] = r * SLOTS + s


def clear_table(table, start, stop):
    for k in range(start, stop):
        table[k] = DEAD


def even_core(columns):
    return (columns[0, 0] // ROWS) % 2 == 0


def pack_kernel(columns, counts, blocks, vectors, swap_far, swap_near, table, zero, sems):
    first = columns[0, 0]
    zero[...] = jnp.zeros_like(zero)
    for r in (0, 1, 2, 3, 28, 29, 30, 31):
        clear_table(table, place(r, -4), place(r, 5))
        fill_table(table, columns, counts, first, r)

    def fill(to_prev, to_next):
        moves = []
        for side, (out, pairs) in enumerate(((to_prev, PAIRS_PREV), (to_next, PAIRS_NEXT))):
            start = 0 if side == 0 else LOCAL - EDGE
            for half in range(2):
                move = pltpu.make_async_copy(
                    vectors.at[pl.ds(start, EDGE), pl.ds(half * B, B)],
                    out.at[pl.ds(10 * B + half * EDGE, EDGE), :],
                    sems.at[side * 12 + 10 + half],
                )
                move.start()
                moves.append(move)
            for k, (r, o) in enumerate(pairs):
                slot = table[place(r, o)]
                target = out.at[pl.ds(k * B, B), :]
                sem = sems.at[side * 12 + k]

                @pl.when(slot < DEAD)
                def _():
                    pltpu.make_async_copy(blocks.at[slot], target, sem).start()

                @pl.when(slot >= DEAD)
                def _():
                    pltpu.make_async_copy(zero, target, sem).start()

                moves.append(pltpu.make_async_copy(zero, target, sem))
        for move in moves:
            move.wait()

    even = even_core(columns)

    @pl.when(even)
    def _():
        fill(swap_far, swap_near)

    @pl.when(jnp.logical_not(even))
    def _():
        fill(swap_near, swap_far)


def window_of(p):
    return max(0, (2 - p) * 2 * B), WIDE - max(0, (p - PANELS + 3) * 2 * B)


def apply_panel(p, hh, hl, vh, vl):
    left, right = window_of(p)
    window = slice(p * 2 * B + left - EDGE, p * 2 * B + right - EDGE)
    high, low = hh[p, :, left:right], hl[p, :, left:right]
    return dot(high, vh[window, :]) + dot(low, vh[window, :]) + dot(high, vl[window, :])


def store_rows(p, value, uh, ul, part):
    at = slice(p * 2 * B, (p + 1) * 2 * B)
    uh[at, :], ul[at, :] = split(value)
    if p < 2:
        part[p * 2 * B : (p + 1) * 2 * B, :] = value
    elif p >= PANELS - 2:
        part[(p - PANELS + 4) * 2 * B : (p - PANELS + 5) * 2 * B, :] = value


def first_kernel(
    columns, counts, blocks, vectors, hh, hl, vh, vl, uh, ul, part, table, sbuf, vbuf, ssem, vsem
):
    def block_copy(r):
        return pltpu.make_async_copy(
            blocks.at[pl.ds(r * SLOTS, SLOTS)],
            sbuf.at[rows((r % RING) * SLOTS, SLOTS)],
            ssem.at[r % RING],
        )

    def vector_copy(q):
        return pltpu.make_async_copy(
            vectors.at[rows(q * 2 * B, 2 * B), :], vbuf.at[q % VRING], vsem.at[q % VRING]
        )

    def take_vectors(q):
        vector_copy(q).wait()
        at = rows(q * 2 * B, 2 * B)
        vh[at, :], vl[at, :] = split(vbuf[q % VRING])

    for r in range(RING):
        block_copy(r).start()
        if r % 2 and r // 2 < VRING:
            vector_copy(r // 2).start()
    sbuf[RING * SLOTS] = jnp.zeros((B, B), F32)
    first = columns[0, 0]

    def clear(r, _):
        for k in range(16):
            table[r * 16 + k] = DEAD
        return 0

    def fill(r, _):
        fill_table(table, columns, counts, first, r)
        return 0

    lax.fori_loop(0, ROWS + 10, clear, 0)
    lax.fori_loop(0, ROWS, fill, 0)

    def fetch(slot):
        return sbuf[jnp.where(slot < DEAD, slot % (RING * SLOTS), RING * SLOTS)]

    def build(p):
        left, right = window_of(p)
        for h in range(2):
            i = 2 * p + h
            at = slice(h * B, h * B + B)
            for c in range(left // B, right // B):
                o = c - 4 - h
                cols = slice(c * B, c * B + B)
                if abs(o) > REACH:
                    parts = (jnp.zeros((B, B), BF16),) * 2
                else:
                    parts = split(fetch(table[place(i, o)]) + fetch(table[place(i + o, -o)]).T)
                hh[p, at, cols], hl[p, at, cols] = parts

    rows_in = vectors_in = 0
    rows_out, vectors_out = RING, VRING
    before = ()
    for group in GROUPS + ((),):
        if group:
            while rows_out < min(ROWS, RING + 2 * group[0] - REACH):
                block_copy(rows_out).start()
                rows_out += 1
            while rows_in < min(ROWS, 2 * group[-1] + 6):
                block_copy(rows_in).wait()
                rows_in += 1
            while vectors_in < min(PANELS, group[-1] + 3):
                take_vectors(vectors_in)
                vectors_in += 1
            while vectors_out < min(PANELS, VRING + vectors_in):
                vector_copy(vectors_out).start()
                vectors_out += 1
        for k in range(max(len(group), len(before))):
            if k < len(group):
                build(group[k])
            if k < len(before):
                store_rows(before[k], 0.5 * apply_panel(before[k], hh, hl, vh, vl), uh, ul, part)
        before = group


def inner_kernel(hh, hl, vh, vl, ph, pr, uh, ul, part):
    for p in range(PANELS):
        at = slice(p * 2 * B, (p + 1) * 2 * B)
        prior = ph[at, :].astype(F32) + pr[at, :].astype(F32)
        store_rows(p, apply_panel(p, hh, hl, vh, vl) - prior, uh, ul, part)


def cross(xh, xl, side, halo_high, halo_low):
    return dot(xh[side], halo_high) + dot(xl[side], halo_high) + dot(xh[side], halo_low)


def write_edge(side, value, uh, ul):
    start = 0 if side == 0 else LOCAL - EDGE
    uh[start : start + EDGE, :], ul[start : start + EDGE, :] = split(value)


def first_edge_kernel(
    columns, sent_far, sent_near, got_far, got_near, part, uh_in, ul_in, *rest
):
    uh, ul, xh, xl, far, near = rest[KEPT:]
    del uh_in, ul_in
    even = even_core(columns)

    def own(side, at):
        a, b = sent_far[at, :], sent_near[at, :]
        return jnp.where(even, a, b) if side == 0 else jnp.where(even, b, a)

    def got(side, at):
        a, b = got_far[at, :], got_near[at, :]
        return jnp.where(even, a, b) if side == 0 else jnp.where(even, b, a)

    zero = jnp.zeros((B, B), BF16)
    for r in range(REACH):
        for c in range(REACH):
            at, cols = slice(r * B, r * B + B), slice(c * B, c * B + B)
            for side in range(2):
                if (c >= r) if side == 0 else (c <= r):
                    if side == 0:
                        a = PAIRS_PREV.index((r, c - 4 - r)) * B
                        b = PAIRS_NEXT.index((28 + c, 4 + r - c)) * B
                    else:
                        a = PAIRS_NEXT.index((28 + r, 4 + c - r)) * B
                        b = PAIRS_PREV.index((c, r - c - 4)) * B
                    parts = split(own(side, slice(a, a + B)) + got(side, slice(b, b + B)).T)
                else:
                    parts = (zero, zero)
                xh[side, at, cols], xl[side, at, cols] = parts
    values = []
    for side in range(2):
        halves = [
            split(got(side, slice(10 * B + half * EDGE, 10 * B + (half + 1) * EDGE)))
            for half in range(2)
        ]
        high = jnp.concatenate([halves[0][0], halves[1][0]], axis=1)
        low = jnp.concatenate([halves[0][1], halves[1][1]], axis=1)
        value = part[side * EDGE : (side + 1) * EDGE, :] + 0.5 * cross(xh, xl, side, high, low)
        write_edge(side, value, uh, ul)
        values.append(value)
    send_edges(even, values, far, near)


def send_edges(even, values, far, near):
    far[...] = jnp.where(even, values[0], values[1])
    near[...] = jnp.where(even, values[1], values[0])


def finish_edges(columns, xh, xl, got_far, got_near, part, uh, ul):
    even = even_core(columns)
    a, b = got_far[...], got_near[...]
    values = []
    for side, halo in enumerate((jnp.where(even, a, b), jnp.where(even, b, a))):
        value = part[side * EDGE : (side + 1) * EDGE, :] + cross(xh, xl, side, *split(halo))
        write_edge(side, value, uh, ul)
        values.append(value)
    return even, values


def edge_kernel(columns, xh, xl, got_far, got_near, part, uh_in, ul_in, *rest):
    uh, ul, far, near = rest[KEPT:]
    del uh_in, ul_in
    even, values = finish_edges(columns, xh, xl, got_far, got_near, part, uh, ul)
    send_edges(even, values, far, near)


def last_edge_kernel(columns, xh, xl, got_far, got_near, part, uh_in, ul_in, uh, ul, mine, theirs):
    del uh_in, ul_in
    even, _ = finish_edges(columns, xh, xl, got_far, got_near, part, uh, ul)
    over = (((0,), (0,)), ((), ()))

    high, low = uh[...], ul[...]
    main = lax.dot_general(high, high, over, preferred_element_type=F32)
    mixed = lax.dot_general(high, low, over, preferred_element_type=F32)
    total = main + mixed + mixed.T
    r = lax.broadcasted_iota(jnp.int32, (B, B), 0)
    c = lax.broadcasted_iota(jnp.int32, (B, B), 1)
    corner, beside = total[B:, B:], total[:B, B:]
    square = jnp.where(c >= r, total[:B, :B], corner)
    diagonal = jnp.broadcast_to(jnp.sum(jnp.where(r == c, corner, 0.0), axis=0, keepdims=True), (8, B))
    none = jnp.zeros((8, B), F32)
    mine[:B, :] = jnp.where(even, square, beside)
    mine[B:, :] = jnp.where(even, diagonal, none)
    theirs[:B, :] = jnp.where(even, beside, square)
    theirs[B:, :] = jnp.where(even, none, diagonal)


def precise(a, b, over=(((1,), (0,)), ((), ()))):
    return lax.dot_general(
        a, b, over, precision=lax.Precision.HIGHEST, preferred_element_type=F32
    )


def close(a, b, over=(((1,), (0,)), ((), ()))):
    (ah, al), (bh, bl) = split(a), split(b)

    def product(x, y):
        return lax.dot_general(x, y, over, preferred_element_type=F32)

    return product(ah, bh) + (product(ah, bl) + product(al, bh))


def basis_kernel(columns, mine, other, uh, ul, scale, basis, factor, work, upper, inverse, out, sems):
    r = lax.broadcasted_iota(jnp.int32, (B, B), 0)
    c = lax.broadcasted_iota(jnp.int32, (B, B), 1)
    even = even_core(columns)
    ad = jnp.where(even, mine[...], other[...])
    b = jnp.where(even, other[:B, :], mine[:B, :])
    square = ad[:B, :]
    high_part = jnp.where(c >= r, square, 0.0)
    low_part = jnp.where(c < r, square, 0.0)
    work[:B, :B] = high_part + jnp.where(c > r, square, 0.0).T
    work[:B, B:] = b
    work[B:, :B] = b.T
    work[B:, B:] = low_part + low_part.T + jnp.where(r == c, ad[B : B + 1, :], 0.0)

    r = lax.broadcasted_iota(jnp.int32, (K, K), 0)
    c = lax.broadcasted_iota(jnp.int32, (K, K), 1)
    gram = work[...]
    eye = jnp.where(r == c, 1.0, 0.0).astype(F32)
    on = jnp.where(r == c, gram, 0.0)
    row_d = jnp.sum(on, axis=0, keepdims=True)
    col_d = jnp.sum(on, axis=1, keepdims=True)
    row_s, col_s = lax.rsqrt(row_d), lax.rsqrt(col_d)
    scaled = gram * row_s * col_s
    work[...] = scaled
    gap = jnp.where(r == c, 0.0, scaled)

    def half_upper(e):
        return jnp.where(c > r, e, jnp.where(c == r, 0.5 * e, 0.0))

    left = (((0,), (0,)), ((), ()))

    def more(state):
        return (state[0] > 1e-6) & (state[0] < 4.0) & (state[1] < 12)

    def newton(state):
        _, count, y = state
        e = close(y, close(scaled, y), left) - eye
        return (jnp.sum(e * e), count + 1, y - close(y, half_upper(e)))

    size, _, y = lax.while_loop(more, newton, (jnp.sum(gap * gap), 0, eye - half_upper(gap)))
    settled = (size <= 1e-6) & (jnp.min(jnp.where(r == c, y, 1.0)) > 0.0)

    @pl.when(settled)
    def _():
        inverse[...] = y
        full = close(y, scaled, left)
        upper[...] = jnp.where(c >= r, full, 0.0)

    @pl.when(jnp.logical_not(settled))
    def _():
        lane = lax.broadcasted_iota(jnp.int32, (1, K), 1)
        down = lax.broadcasted_iota(jnp.int32, (K, 1), 0)

        def column(k, _):
            a = work[...]
            row = work[pl.ds(k, 1), :]
            root = lax.rsqrt(jnp.sum(jnp.where(lane == k, row, 0.0)))
            row = jnp.where(lane >= k, row * root, 0.0)
            col = jnp.sum(jnp.where(c == k, a, 0.0), axis=1, keepdims=True)
            col = jnp.where(down >= k, col * root, 0.0)
            upper[pl.ds(k, 1), :] = row
            work[...] = a - col * row
            return 0

        lax.fori_loop(0, K, column, 0)
        inverse[...] = jnp.zeros((K, K), F32)

        def back(t, _):
            k = K - 1 - t
            row = upper[pl.ds(k, 1), :]
            pivot = jnp.sum(jnp.where(lane == k, row, 0.0))
            rest = jnp.broadcast_to(jnp.where(lane > k, row, 0.0), (8, K))
            known = precise(rest, inverse[...])[:1, :]
            inverse[pl.ds(k, 1), :] = (jnp.where(lane == k, 1.0, 0.0) - known) / pivot
            return 0

        lax.fori_loop(0, K, back, 0)

    root = scale[0]
    factor[...] = upper[...] * (row_d * row_s) / root
    wh, wl = split(inverse[...] * (col_s * root))

    def out_copy(q):
        at = rows(q * CHUNK, CHUNK)
        return pltpu.make_async_copy(out.at[at, :], basis.at[at, :], sems.at[q])

    def step(q, _):
        at = rows(q * CHUNK, CHUNK)
        out[at, :] = dot(uh[at, :], wh) + dot(ul[at, :], wh) + dot(uh[at, :], wl)
        out_copy(q).start()
        return 0

    lax.fori_loop(0, LOCAL // CHUNK, step, 0)
    for q in range(LOCAL // CHUNK):
        out_copy(q).wait()


def swap_pairs(far, near):
    count = lax.axis_size(ALL)
    pairs = [(i, i + 1) for i in range(1, count - 1, 2)]
    got_far = lax.ppermute(far, ALL, pairs + [(j, i) for i, j in pairs])
    got_near = lax.ppermute(near, "c", [(0, 1), (1, 0)])
    return got_far, got_near


def group_sum(value, axis):
    count = lax.axis_size(axis)
    one, two, three = (
        lax.ppermute(value, axis, [(i, i ^ k) for i in range(count)]) for k in (1, 2, 3)
    )
    return (value + one) + (two + three)


def body(blocks, columns, counts, start_vectors):
    flat, start_vectors, counts, columns = (
        pltpu.with_memory_space_constraint(x, pltpu.HBM)
        for x in (blocks.reshape(DEAD, B, B), start_vectors, counts, columns.T)
    )
    packed = pltpu.VMEM((PACKED, B), F32)
    sent = pl.pallas_call(
        pack_kernel,
        out_shape=(packed, packed),
        in_specs=(SM, SM, HB, HB),
        out_specs=(VM, VM),
        scratch_shapes=[
            pltpu.SMEM((TABLE + 1,), jnp.int32),
            pltpu.VMEM((B, B), F32),
            pltpu.SemaphoreType.DMA((24,)),
        ],
        compiler_params=params(2),
        cost_estimate=cost(0, 2 * 2 * PACKED * B * 4),
        name="pack_edges",
    )(columns, counts, flat, start_vectors)
    got = swap_pairs(*sent)

    wide = pltpu.VMEM((PANELS, 2 * B, WIDE), BF16)
    slab = pltpu.VMEM((LOCAL, K), BF16)
    partial = pltpu.VMEM((2 * EDGE, K), F32)
    crossing = pltpu.VMEM((2, EDGE, EDGE), BF16)
    edge = jax.ShapeDtypeStruct((EDGE, K), F32)
    flops = 3 * 2 * PANELS * 2 * B * WIDE * K
    hh, hl, vh, vl, uh, ul, part = pl.pallas_call(
        first_kernel,
        out_shape=(wide, wide, slab, slab, slab, slab, partial),
        in_specs=(SM, SM, HB, HB),
        out_specs=(VM,) * 7,
        scratch_shapes=[
            pltpu.SMEM((TABLE + 1,), jnp.int32),
            pltpu.VMEM((RING * SLOTS + 1, B, B), F32),
            pltpu.VMEM((VRING, 2 * B, K), F32),
        ]
        + [pltpu.SemaphoreType.DMA((RING,)), pltpu.SemaphoreType.DMA((VRING,))],
        compiler_params=params(16),
        cost_estimate=cost(flops * 2, 24 * 2**20),
        name="first_inner",
    )(columns, counts, flat, start_vectors)

    uh, ul, xh, xl, far, near = pl.pallas_call(
        first_edge_kernel,
        out_shape=(slab, slab, crossing, crossing, edge, edge),
        in_specs=(SM,) + (VM,) * (7 + KEPT),
        out_specs=(VM,) * 6,
        input_output_aliases={6: 0, 7: 1},
        compiler_params=params(4),
        cost_estimate=cost(8e8, 6 * 2**20),
        name="first_edge",
    )(columns, *sent, *got, part, uh, ul, hh, hl, vh, vl)

    def inner(vectors, prior):
        return pl.pallas_call(
            inner_kernel,
            out_shape=(slab, slab, partial),
            in_specs=(VM,) * 6,
            out_specs=(VM,) * 3,
            compiler_params=params(6),
            cost_estimate=cost(flops, 2**20),
            name="inner",
        )(hh, hl, *vectors, *prior)

    got = swap_pairs(far, near)
    wh, wl, part = inner((uh, ul), (vh, vl))
    wh, wl, far, near = pl.pallas_call(
        edge_kernel,
        out_shape=(slab, slab, edge, edge),
        in_specs=(SM,) + (VM,) * (7 + KEPT),
        out_specs=(VM,) * 4,
        input_output_aliases={6: 0, 7: 1},
        compiler_params=params(8),
        cost_estimate=cost(8e8, 2 * 2**20),
        name="edge",
    )(columns, xh, xl, *got, part, wh, wl, hh, hl, uh, ul)

    got = swap_pairs(far, near)
    fh, fl, part = inner((wh, wl), (uh, ul))
    half = pltpu.VMEM((B + 8, B), F32)
    fh, fl, mine, theirs = pl.pallas_call(
        last_edge_kernel,
        out_shape=(slab, slab, half, half),
        in_specs=(SM,) + (VM,) * 7,
        out_specs=(VM,) * 4,
        input_output_aliases={6: 0, 7: 1},
        compiler_params=params(8),
        cost_estimate=cost(2e9, 2 * 2**20),
        name="last_edge_gram",
    )(columns, xh, xl, *got, part, fh, fl)

    swap = [(0, 1), (1, 0)]
    mine = mine + lax.ppermute(theirs, "c", swap)
    for axis in ("y", "x", "z"):
        mine = group_sum(mine, axis)
    other = lax.ppermute(mine, "c", swap)

    total_rows = LOCAL * lax.axis_size(ALL)
    scale = jnp.sqrt(jnp.float32(total_rows)).reshape(1)
    basis, factor = pl.pallas_call(
        basis_kernel,
        out_shape=(jax.ShapeDtypeStruct((LOCAL, K), F32), jax.ShapeDtypeStruct((K, K), F32)),
        in_specs=(SM, VM, VM, VM, VM, SM),
        out_specs=(HB, VM),
        scratch_shapes=[pltpu.VMEM((K, K), F32)] * 3
        + [pltpu.VMEM((LOCAL, K), F32), pltpu.SemaphoreType.DMA((LOCAL // CHUNK,))],
        compiler_params=params(12),
        cost_estimate=cost(2e9, 4 * 2**20),
        name="basis",
    )(columns, mine, other, fh, fl, scale)
    return basis, factor


def solution(mesh):
    fine = Mesh(mesh.devices.reshape(4, 4, 4, 2), ALL)
    placed = (P(ALL, None, None, None), P(ALL, None), P(ALL), P(ALL, None))
    return jax.shard_map(
        body, mesh=fine, in_specs=placed, out_specs=(P(ALL, None), P()), check_vma=False
    )
```

```python
import jax
import jax.numpy as jnp
from jax import lax
from jax.experimental import pallas as pl
from jax.experimental.pallas import tpu as pltpu
from jax.sharding import Mesh, PartitionSpec as P

B = 128
K = 256
ROWS = 32
SLOTS = 8
REACH = 4
PANELS = ROWS // 2
WIDE = 10 * B
EDGE = REACH * B
LOCAL = ROWS * B
DEAD = ROWS * SLOTS
TABLE = (ROWS + 10) * 16
RING = 24
VRING = 8
GROUPS = ((0, 1), (2, 3, 4, 5), (6, 7, 8, 9), (10, 11, 12, 13), (14, 15))
KEPT = 4
CHUNK = 2048
PAIRS_PREV = [(r, o) for r in range(4) for o in range(-4, 0) if r + o < 0]
PAIRS_NEXT = [(r, o) for r in range(28, 32) for o in range(1, 5) if r + o > 31]
PACKED = 10 * B + 2 * EDGE

F32 = jnp.float32
BF16 = jnp.bfloat16
VM = pl.BlockSpec(memory_space=pltpu.VMEM)
SM = pl.BlockSpec(memory_space=pltpu.SMEM)
HB = pl.BlockSpec(memory_space=pltpu.HBM)
ALL = ("y", "x", "z", "c")


def params(mib):
    return pltpu.CompilerParams(vmem_limit_bytes=mib * 2**20)


def cost(flops, moved):
    return pl.CostEstimate(flops=int(flops), bytes_accessed=int(moved), transcendentals=0)


def dot(a, b):
    return jnp.dot(a, b, preferred_element_type=F32)


def split(x):
    high = x.astype(BF16)
    return high, (x - high.astype(F32)).astype(BF16)


def rows(start, size):
    return pl.ds(pl.multiple_of(start, size), size)


def place(r, o):
    return (r + 5) * 16 + o + 5


def fill_table(table, columns, counts, first, r):
    for s in range(SLOTS):
        offset = columns[s, r] - first - r
        table[jnp.where(s < counts[r], place(r, offset), TABLE)] = r * SLOTS + s


def clear_table(table, start, stop):
    for k in range(start, stop):
        table[k] = DEAD


def even_core(columns):
    return (columns[0, 0] // ROWS) % 2 == 0


def pack_kernel(columns, counts, blocks, vectors, swap_far, swap_near, table, zero, sems):
    first = columns[0, 0]
    zero[...] = jnp.zeros_like(zero)
    for r in (0, 1, 2, 3, 28, 29, 30, 31):
        clear_table(table, place(r, -4), place(r, 5))
        fill_table(table, columns, counts, first, r)

    def fill(to_prev, to_next):
        moves = []
        for side, (out, pairs) in enumerate(((to_prev, PAIRS_PREV), (to_next, PAIRS_NEXT))):
            start = 0 if side == 0 else LOCAL - EDGE
            for half in range(2):
                move = pltpu.make_async_copy(
                    vectors.at[pl.ds(start, EDGE), pl.ds(half * B, B)],
                    out.at[pl.ds(10 * B + half * EDGE, EDGE), :],
                    sems.at[side * 12 + 10 + half],
                )
                move.start()
                moves.append(move)
            for k, (r, o) in enumerate(pairs):
                slot = table[place(r, o)]
                target = out.at[pl.ds(k * B, B), :]
                sem = sems.at[side * 12 + k]

                @pl.when(slot < DEAD)
                def _():
                    pltpu.make_async_copy(blocks.at[slot], target, sem).start()

                @pl.when(slot >= DEAD)
                def _():
                    pltpu.make_async_copy(zero, target, sem).start()

                moves.append(pltpu.make_async_copy(zero, target, sem))
        for move in moves:
            move.wait()

    even = even_core(columns)

    @pl.when(even)
    def _():
        fill(swap_far, swap_near)

    @pl.when(jnp.logical_not(even))
    def _():
        fill(swap_near, swap_far)


def window_of(p):
    return max(0, (2 - p) * 2 * B), WIDE - max(0, (p - PANELS + 3) * 2 * B)


def apply_panel(p, hh, hl, vh, vl):
    left, right = window_of(p)
    window = slice(p * 2 * B + left - EDGE, p * 2 * B + right - EDGE)
    high, low = hh[p, :, left:right], hl[p, :, left:right]
    return dot(high, vh[window, :]) + dot(low, vh[window, :]) + dot(high, vl[window, :])


def store_rows(p, value, uh, ul, part):
    at = slice(p * 2 * B, (p + 1) * 2 * B)
    uh[at, :], ul[at, :] = split(value)
    if p < 2:
        part[p * 2 * B : (p + 1) * 2 * B, :] = value
    elif p >= PANELS - 2:
        part[(p - PANELS + 4) * 2 * B : (p - PANELS + 5) * 2 * B, :] = value


def first_kernel(
    columns, counts, blocks, vectors, hh, hl, vh, vl, uh, ul, part, table, sbuf, vbuf, ssem, vsem
):
    class block_copy:
        def __init__(self, r):
            self.more = counts[r] > SLOTS // 2
            self.parts = [
                pltpu.make_async_copy(
                    blocks.at[pl.ds(r * SLOTS + k * 4, SLOTS // 2)],
                    sbuf.at[pl.ds((r % RING) * SLOTS + k * 4, SLOTS // 2)],
                    ssem.at[r % RING, k],
                )
                for k in range(2)
            ]

        def start(self):
            self.parts[0].start()
            pl.when(self.more)(self.parts[1].start)

        def wait(self):
            self.parts[0].wait()
            pl.when(self.more)(self.parts[1].wait)

    def vector_copy(q):
        return pltpu.make_async_copy(
            vectors.at[rows(q * 2 * B, 2 * B), :], vbuf.at[q % VRING], vsem.at[q % VRING]
        )

    def take_vectors(q):
        vector_copy(q).wait()
        at = rows(q * 2 * B, 2 * B)
        vh[at, :], vl[at, :] = split(vbuf[q % VRING])

    for r in range(RING):
        block_copy(r).start()
        if r % 2 and r // 2 < VRING:
            vector_copy(r // 2).start()
    sbuf[RING * SLOTS] = jnp.zeros((B, B), F32)
    first = columns[0, 0]

    def clear(r, _):
        for k in range(16):
            table[r * 16 + k] = DEAD
        return 0

    def fill(r, _):
        fill_table(table, columns, counts, first, r)
        return 0

    lax.fori_loop(0, ROWS + 10, clear, 0)
    lax.fori_loop(0, ROWS, fill, 0)

    def fetch(slot):
        return sbuf[jnp.where(slot < DEAD, slot % (RING * SLOTS), RING * SLOTS)]

    def build(p):
        left, right = window_of(p)
        for h in range(2):
            i = 2 * p + h
            at = slice(h * B, h * B + B)
            for c in range(left // B, right // B):
                o = c - 4 - h
                cols = slice(c * B, c * B + B)
                if abs(o) > REACH:
                    parts = (jnp.zeros((B, B), BF16),) * 2
                else:
                    parts = split(fetch(table[place(i, o)]) + fetch(table[place(i + o, -o)]).T)
                hh[p, at, cols], hl[p, at, cols] = parts

    rows_in = vectors_in = 0
    rows_out, vectors_out = RING, VRING
    before = ()
    for group in GROUPS + ((),):
        if group:
            while rows_out < min(ROWS, RING + 2 * group[0] - REACH):
                block_copy(rows_out).start()
                rows_out += 1
            while rows_in < min(ROWS, 2 * group[-1] + 6):
                block_copy(rows_in).wait()
                rows_in += 1
            while vectors_in < min(PANELS, group[-1] + 3):
                take_vectors(vectors_in)
                vectors_in += 1
            while vectors_out < min(PANELS, VRING + vectors_in):
                vector_copy(vectors_out).start()
                vectors_out += 1
        for k in range(max(len(group), len(before))):
            if k < len(group):
                build(group[k])
            if k < len(before):
                store_rows(before[k], 0.5 * apply_panel(before[k], hh, hl, vh, vl), uh, ul, part)
        before = group


def inner_kernel(hh, hl, vh, vl, ph, pr, uh, ul, part, *gram):
    for p in range(PANELS):
        at = slice(p * 2 * B, (p + 1) * 2 * B)
        prior = ph[at, :].astype(F32) + pr[at, :].astype(F32)
        store_rows(p, apply_panel(p, hh, hl, vh, vl) - prior, uh, ul, part)
    if gram:
        gram[0][0], gram[0][1] = gram_parts(slice(EDGE, LOCAL - EDGE), uh, ul)


def gram_parts(at, high, low):
    over = (((0,), (0,)), ((), ()))
    flipped = high[at, :]
    return (
        lax.dot_general(flipped, high[at, :], over, preferred_element_type=F32),
        lax.dot_general(flipped, low[at, :], over, preferred_element_type=F32),
    )


def cross(xh, xl, side, halo_high, halo_low):
    return dot(xh[side], halo_high) + dot(xl[side], halo_high) + dot(xh[side], halo_low)


def write_edge(side, value, uh, ul):
    start = 0 if side == 0 else LOCAL - EDGE
    uh[start : start + EDGE, :], ul[start : start + EDGE, :] = split(value)


def first_edge_kernel(
    columns, sent_far, sent_near, got_far, got_near, part, uh_in, ul_in, *rest
):
    uh, ul, xh, xl, far, near = rest[KEPT:]
    del uh_in, ul_in
    even = even_core(columns)

    def own(side, at):
        a, b = sent_far[at, :], sent_near[at, :]
        return jnp.where(even, a, b) if side == 0 else jnp.where(even, b, a)

    def got(side, at):
        a, b = got_far[at, :], got_near[at, :]
        return jnp.where(even, a, b) if side == 0 else jnp.where(even, b, a)

    zero = jnp.zeros((B, B), BF16)
    for r in range(REACH):
        for c in range(REACH):
            at, cols = slice(r * B, r * B + B), slice(c * B, c * B + B)
            for side in range(2):
                if (c >= r) if side == 0 else (c <= r):
                    if side == 0:
                        a = PAIRS_PREV.index((r, c - 4 - r)) * B
                        b = PAIRS_NEXT.index((28 + c, 4 + r - c)) * B
                    else:
                        a = PAIRS_NEXT.index((28 + r, 4 + c - r)) * B
                        b = PAIRS_PREV.index((c, r - c - 4)) * B
                    parts = split(own(side, slice(a, a + B)) + got(side, slice(b, b + B)).T)
                else:
                    parts = (zero, zero)
                xh[side, at, cols], xl[side, at, cols] = parts
    values = []
    for side in range(2):
        halves = [
            split(got(side, slice(10 * B + half * EDGE, 10 * B + (half + 1) * EDGE)))
            for half in range(2)
        ]
        high = jnp.concatenate([halves[0][0], halves[1][0]], axis=1)
        low = jnp.concatenate([halves[0][1], halves[1][1]], axis=1)
        value = part[side * EDGE : (side + 1) * EDGE, :] + 0.5 * cross(xh, xl, side, high, low)
        write_edge(side, value, uh, ul)
        values.append(value)
    send_edges(even, values, far, near)


def send_edges(even, values, far, near):
    far[...] = jnp.where(even, values[0], values[1])
    near[...] = jnp.where(even, values[1], values[0])


def finish_edges(columns, xh, xl, got_far, got_near, part, uh, ul):
    even = even_core(columns)
    a, b = got_far[...], got_near[...]
    values = []
    for side, halo in enumerate((jnp.where(even, a, b), jnp.where(even, b, a))):
        value = part[side * EDGE : (side + 1) * EDGE, :] + cross(xh, xl, side, *split(halo))
        write_edge(side, value, uh, ul)
        values.append(value)
    return even, values


def edge_kernel(columns, xh, xl, got_far, got_near, part, uh_in, ul_in, *rest):
    uh, ul, far, near = rest[KEPT:]
    del uh_in, ul_in
    even, values = finish_edges(columns, xh, xl, got_far, got_near, part, uh, ul)
    send_edges(even, values, far, near)


def last_edge_kernel(columns, xh, xl, got_far, got_near, part, uh_in, ul_in, inside, uh, ul, mine, theirs):
    del uh_in, ul_in
    even, _ = finish_edges(columns, xh, xl, got_far, got_near, part, uh, ul)
    first = gram_parts(slice(0, EDGE), uh, ul)
    last = gram_parts(slice(LOCAL - EDGE, LOCAL), uh, ul)
    main, mixed = (inside[k] + (first[k] + last[k]) for k in range(2))
    total = main + mixed + mixed.T
    r = lax.broadcasted_iota(jnp.int32, (B, B), 0)
    c = lax.broadcasted_iota(jnp.int32, (B, B), 1)
    corner, beside = total[B:, B:], total[:B, B:]
    square = jnp.where(c >= r, total[:B, :B], corner)
    diagonal = jnp.broadcast_to(jnp.sum(jnp.where(r == c, corner, 0.0), axis=0, keepdims=True), (8, B))
    none = jnp.zeros((8, B), F32)
    mine[:B, :] = jnp.where(even, square, beside)
    mine[B:, :] = jnp.where(even, diagonal, none)
    theirs[:B, :] = jnp.where(even, beside, square)
    theirs[B:, :] = jnp.where(even, none, diagonal)


def precise(a, b, over=(((1,), (0,)), ((), ()))):
    return lax.dot_general(
        a, b, over, precision=lax.Precision.HIGHEST, preferred_element_type=F32
    )


def close(a, b, over=(((1,), (0,)), ((), ()))):
    (ah, al), (bh, bl) = split(a), split(b)

    def product(x, y):
        return lax.dot_general(x, y, over, preferred_element_type=F32)

    return product(ah, bh) + (product(ah, bl) + product(al, bh))


def basis_kernel(columns, mine, other, uh, ul, scale, basis, factor, work, upper, inverse, out, sems):
    r = lax.broadcasted_iota(jnp.int32, (B, B), 0)
    c = lax.broadcasted_iota(jnp.int32, (B, B), 1)
    even = even_core(columns)
    ad = jnp.where(even, mine[...], other[...])
    b = jnp.where(even, other[:B, :], mine[:B, :])
    square = ad[:B, :]
    high_part = jnp.where(c >= r, square, 0.0)
    low_part = jnp.where(c < r, square, 0.0)
    work[:B, :B] = high_part + jnp.where(c > r, square, 0.0).T
    work[:B, B:] = b
    work[B:, :B] = b.T
    work[B:, B:] = low_part + low_part.T + jnp.where(r == c, ad[B : B + 1, :], 0.0)

    r = lax.broadcasted_iota(jnp.int32, (K, K), 0)
    c = lax.broadcasted_iota(jnp.int32, (K, K), 1)
    gram = work[...]
    eye = jnp.where(r == c, 1.0, 0.0).astype(F32)
    on = jnp.where(r == c, gram, 0.0)
    row_d = jnp.sum(on, axis=0, keepdims=True)
    col_d = jnp.sum(on, axis=1, keepdims=True)
    row_s, col_s = lax.rsqrt(row_d), lax.rsqrt(col_d)
    scaled = gram * row_s * col_s
    work[...] = scaled
    gap = jnp.where(r == c, 0.0, scaled)

    def half_upper(e):
        return jnp.where(c > r, e, jnp.where(c == r, 0.5 * e, 0.0))

    left = (((0,), (0,)), ((), ()))

    def measured(y):
        e = close(y, close(scaled, y), left) - eye
        return jnp.sum(e * e), e, y

    def more(state):
        return (state[0] > 1e-7) & (state[0] < 4.0) & (state[3] < 12)

    def newton(state):
        _, e, y, count = state
        return (*measured(y - close(y, half_upper(e))), count + 1)

    size, _, y, _ = lax.while_loop(more, newton, (*measured(eye - half_upper(gap)), 0))
    settled = (size <= 1e-7) & (jnp.min(jnp.where(r == c, y, 1.0)) > 0.0)

    @pl.when(settled)
    def _():
        inverse[...] = y
        full = close(y, scaled, left)
        upper[...] = jnp.where(c >= r, full, 0.0)

    @pl.when(jnp.logical_not(settled))
    def _():
        lane = lax.broadcasted_iota(jnp.int32, (1, K), 1)
        down = lax.broadcasted_iota(jnp.int32, (K, 1), 0)

        def column(k, _):
            a = work[...]
            row = work[pl.ds(k, 1), :]
            root = lax.rsqrt(jnp.sum(jnp.where(lane == k, row, 0.0)))
            row = jnp.where(lane >= k, row * root, 0.0)
            col = jnp.sum(jnp.where(c == k, a, 0.0), axis=1, keepdims=True)
            col = jnp.where(down >= k, col * root, 0.0)
            upper[pl.ds(k, 1), :] = row
            work[...] = a - col * row
            return 0

        lax.fori_loop(0, K, column, 0)
        inverse[...] = jnp.zeros((K, K), F32)

        def back(t, _):
            k = K - 1 - t
            row = upper[pl.ds(k, 1), :]
            pivot = jnp.sum(jnp.where(lane == k, row, 0.0))
            rest = jnp.broadcast_to(jnp.where(lane > k, row, 0.0), (8, K))
            known = precise(rest, inverse[...])[:1, :]
            inverse[pl.ds(k, 1), :] = (jnp.where(lane == k, 1.0, 0.0) - known) / pivot
            return 0

        lax.fori_loop(0, K, back, 0)

    root = scale[0]
    factor[...] = upper[...] * (row_d * row_s) / root
    wh, wl = split(inverse[...] * (col_s * root))

    def out_copy(q):
        at = rows(q * CHUNK, CHUNK)
        return pltpu.make_async_copy(out.at[at, :], basis.at[at, :], sems.at[q])

    def step(q, _):
        at = rows(q * CHUNK, CHUNK)
        out[at, :] = dot(uh[at, :], wh) + dot(ul[at, :], wh) + dot(uh[at, :], wl)
        out_copy(q).start()
        return 0

    lax.fori_loop(0, LOCAL // CHUNK, step, 0)
    for q in range(LOCAL // CHUNK):
        out_copy(q).wait()


def swap_pairs(far, near):
    count = lax.axis_size(ALL)
    pairs = [(i, i + 1) for i in range(1, count - 1, 2)]
    got_far = lax.ppermute(far, ALL, pairs + [(j, i) for i, j in pairs])
    got_near = lax.ppermute(near, "c", [(0, 1), (1, 0)])
    return got_far, got_near


def group_sum(value, axis):
    count = lax.axis_size(axis)
    one, two, three = (
        lax.ppermute(value, axis, [(i, i ^ k) for i in range(count)]) for k in (1, 2, 3)
    )
    return (value + one) + (two + three)


def body(blocks, columns, counts, start_vectors):
    flat, start_vectors, counts, columns = (
        pltpu.with_memory_space_constraint(x, pltpu.HBM)
        for x in (blocks.reshape(DEAD, B, B), start_vectors, counts, columns.T)
    )
    packed = pltpu.VMEM((PACKED, B), F32)
    sent = pl.pallas_call(
        pack_kernel,
        out_shape=(packed, packed),
        in_specs=(SM, SM, HB, HB),
        out_specs=(VM, VM),
        scratch_shapes=[
            pltpu.SMEM((TABLE + 1,), jnp.int32),
            pltpu.VMEM((B, B), F32),
            pltpu.SemaphoreType.DMA((24,)),
        ],
        compiler_params=params(2),
        cost_estimate=cost(0, 2 * 2 * PACKED * B * 4),
        name="pack_edges",
    )(columns, counts, flat, start_vectors)
    got = swap_pairs(*sent)

    wide = pltpu.VMEM((PANELS, 2 * B, WIDE), BF16)
    slab = pltpu.VMEM((LOCAL, K), BF16)
    partial = pltpu.VMEM((2 * EDGE, K), F32)
    crossing = pltpu.VMEM((2, EDGE, EDGE), BF16)
    edge = jax.ShapeDtypeStruct((EDGE, K), F32)
    flops = 3 * 2 * PANELS * 2 * B * WIDE * K
    hh, hl, vh, vl, uh, ul, part = pl.pallas_call(
        first_kernel,
        out_shape=(wide, wide, slab, slab, slab, slab, partial),
        in_specs=(SM, SM, HB, HB),
        out_specs=(VM,) * 7,
        scratch_shapes=[
            pltpu.SMEM((TABLE + 1,), jnp.int32),
            pltpu.VMEM((RING * SLOTS + 1, B, B), F32),
            pltpu.VMEM((VRING, 2 * B, K), F32),
        ]
        + [pltpu.SemaphoreType.DMA((RING, 2)), pltpu.SemaphoreType.DMA((VRING,))],
        compiler_params=params(16),
        cost_estimate=cost(flops * 2, 24 * 2**20),
        name="first_inner",
    )(columns, counts, flat, start_vectors)

    uh, ul, xh, xl, far, near = pl.pallas_call(
        first_edge_kernel,
        out_shape=(slab, slab, crossing, crossing, edge, edge),
        in_specs=(SM,) + (VM,) * (7 + KEPT),
        out_specs=(VM,) * 6,
        input_output_aliases={6: 0, 7: 1},
        compiler_params=params(4),
        cost_estimate=cost(8e8, 6 * 2**20),
        name="first_edge",
    )(columns, *sent, *got, part, uh, ul, hh, hl, vh, vl)

    def inner(vectors, prior, *gram):
        return pl.pallas_call(
            inner_kernel,
            out_shape=(slab, slab, partial) + gram,
            in_specs=(VM,) * 6,
            out_specs=(VM,) * (3 + len(gram)),
            compiler_params=params(6),
            cost_estimate=cost(flops, 2**20),
            name="inner",
        )(hh, hl, *vectors, *prior)

    got = swap_pairs(far, near)
    wh, wl, part = inner((uh, ul), (vh, vl))
    wh, wl, far, near = pl.pallas_call(
        edge_kernel,
        out_shape=(slab, slab, edge, edge),
        in_specs=(SM,) + (VM,) * (7 + KEPT),
        out_specs=(VM,) * 4,
        input_output_aliases={6: 0, 7: 1},
        compiler_params=params(8),
        cost_estimate=cost(8e8, 2 * 2**20),
        name="edge",
    )(columns, xh, xl, *got, part, wh, wl, hh, hl, uh, ul)

    got = swap_pairs(far, near)
    fh, fl, part, inside = inner((wh, wl), (uh, ul), pltpu.VMEM((2, K, K), F32))
    half = pltpu.VMEM((B + 8, B), F32)
    fh, fl, mine, theirs = pl.pallas_call(
        last_edge_kernel,
        out_shape=(slab, slab, half, half),
        in_specs=(SM,) + (VM,) * 8,
        out_specs=(VM,) * 4,
        input_output_aliases={6: 0, 7: 1},
        compiler_params=params(8),
        cost_estimate=cost(2e9, 2 * 2**20),
        name="last_edge_gram",
    )(columns, xh, xl, *got, part, fh, fl, inside)

    swap = [(0, 1), (1, 0)]
    mine = mine + lax.ppermute(theirs, "c", swap)
    for axis in ("y", "x", "z"):
        mine = group_sum(mine, axis)
    other = lax.ppermute(mine, "c", swap)

    total_rows = LOCAL * lax.axis_size(ALL)
    scale = jnp.sqrt(jnp.float32(total_rows)).reshape(1)
    basis, factor = pl.pallas_call(
        basis_kernel,
        out_shape=(jax.ShapeDtypeStruct((LOCAL, K), F32), jax.ShapeDtypeStruct((K, K), F32)),
        in_specs=(SM, VM, VM, VM, VM, SM),
        out_specs=(HB, VM),
        scratch_shapes=[pltpu.VMEM((K, K), F32)] * 3
        + [pltpu.VMEM((LOCAL, K), F32), pltpu.SemaphoreType.DMA((LOCAL // CHUNK,))],
        compiler_params=params(12),
        cost_estimate=cost(2e9, 4 * 2**20),
        name="basis",
    )(columns, mine, other, fh, fl, scale)
    return basis, factor


def solution(mesh):
    fine = Mesh(mesh.devices.reshape(4, 4, 4, 2), ALL)
    placed = (P(ALL, None, None, None), P(ALL, None), P(ALL), P(ALL, None))
    return jax.shard_map(
        body, mesh=fine, in_specs=placed, out_specs=(P(ALL, None), P()), check_vma=False
    )
```

```python
import functools
import math

import jax
import jax.numpy as jnp
from jax import lax
from jax.experimental import pallas as pl
from jax.experimental.pallas import tpu as pltpu
from jax.sharding import Mesh, PartitionSpec as P

B = 128
K = 256
ROWS = 32
SLOTS = 8
REACH = 4
PANELS = ROWS // 2
WIDE = 10 * B
EDGE = REACH * B
LOCAL = ROWS * B
DEAD = ROWS * SLOTS
TABLE = (ROWS + 10) * 16
RING = 24
VRING = 8
GROUPS = ((0, 1), (2, 3, 4, 5), (6, 7, 8, 9), (10, 11, 12, 13), (14, 15))
KEPT = 4
CHUNK = 2048
PAIRS_PREV = [(r, o) for r in range(4) for o in range(-4, 0) if r + o < 0]
PAIRS_NEXT = [(r, o) for r in range(28, 32) for o in range(1, 5) if r + o > 31]
PACKED = 10 * B + 2 * EDGE

F32 = jnp.float32
BF16 = jnp.bfloat16
VM = pl.BlockSpec(memory_space=pltpu.VMEM)
SM = pl.BlockSpec(memory_space=pltpu.SMEM)
HB = pl.BlockSpec(memory_space=pltpu.HBM)
ALL = ("y", "x", "z", "c")


def params(mib):
    return pltpu.CompilerParams(vmem_limit_bytes=mib * 2**20)


def cost(flops, moved):
    return pl.CostEstimate(flops=int(flops), bytes_accessed=int(moved), transcendentals=0)


def dot(a, b):
    return jnp.dot(a, b, preferred_element_type=F32)


def split(x):
    high = x.astype(BF16)
    return high, (x - high.astype(F32)).astype(BF16)


def rows(start, size):
    return pl.ds(pl.multiple_of(start, size), size)


def place(r, o):
    return (r + 5) * 16 + o + 5


def fill_table(table, columns, counts, first, r):
    for s in range(SLOTS):
        offset = columns[s, r] - first - r
        table[jnp.where(s < counts[r], place(r, offset), TABLE)] = r * SLOTS + s


def clear_table(table, start, stop):
    for k in range(start, stop):
        table[k] = DEAD


def even_core():
    return lax.axis_index("c") == 0


def pack_kernel(columns, counts, blocks, vectors, swap_far, swap_near, table, zero, sems):
    first = columns[0, 0]
    zero[...] = jnp.zeros_like(zero)
    for r in (0, 1, 2, 3, 28, 29, 30, 31):
        clear_table(table, place(r, -4), place(r, 5))
        fill_table(table, columns, counts, first, r)

    def fill(to_prev, to_next):
        moves = []
        for side, (out, pairs) in enumerate(((to_prev, PAIRS_PREV), (to_next, PAIRS_NEXT))):
            start = 0 if side == 0 else LOCAL - EDGE
            for half in range(2):
                move = pltpu.make_async_copy(
                    vectors.at[pl.ds(start, EDGE), pl.ds(half * B, B)],
                    out.at[pl.ds(10 * B + half * EDGE, EDGE), :],
                    sems.at[side * 12 + 10 + half],
                )
                move.start()
                moves.append(move)
            for k, (r, o) in enumerate(pairs):
                slot = table[place(r, o)]
                target = out.at[pl.ds(k * B, B), :]
                sem = sems.at[side * 12 + k]

                @pl.when(slot < DEAD)
                def _():
                    pltpu.make_async_copy(blocks.at[slot], target, sem).start()

                @pl.when(slot >= DEAD)
                def _():
                    pltpu.make_async_copy(zero, target, sem).start()

                moves.append(pltpu.make_async_copy(zero, target, sem))
        for move in moves:
            move.wait()

    even = even_core()

    @pl.when(even)
    def _():
        fill(swap_far, swap_near)

    @pl.when(jnp.logical_not(even))
    def _():
        fill(swap_near, swap_far)


def window_of(p):
    return max(0, (2 - p) * 2 * B), WIDE - max(0, (p - PANELS + 3) * 2 * B)


def apply_panel(p, hh, hl, vh, vl):
    left, right = window_of(p)
    window = slice(p * 2 * B + left - EDGE, p * 2 * B + right - EDGE)
    high, low = hh[p, :, left:right], hl[p, :, left:right]
    return dot(high, vh[window, :]) + dot(low, vh[window, :]) + dot(high, vl[window, :])


def store_rows(p, value, uh, ul, part):
    at = slice(p * 2 * B, (p + 1) * 2 * B)
    uh[at, :], ul[at, :] = split(value)
    if p < 2:
        part[p * 2 * B : (p + 1) * 2 * B, :] = value
    elif p >= PANELS - 2:
        part[(p - PANELS + 4) * 2 * B : (p - PANELS + 5) * 2 * B, :] = value


def first_kernel(
    columns, counts, blocks, vectors, hh, hl, vh, vl, uh, ul, part, table, sbuf, vbuf, ssem, vsem
):
    class block_copy:
        def __init__(self, r):
            self.more = counts[r] > SLOTS // 2
            self.parts = [
                pltpu.make_async_copy(
                    blocks.at[pl.ds(r * SLOTS + k * 4, SLOTS // 2)],
                    sbuf.at[pl.ds((r % RING) * SLOTS + k * 4, SLOTS // 2)],
                    ssem.at[r % RING, k],
                )
                for k in range(2)
            ]

        def start(self):
            self.parts[0].start()
            pl.when(self.more)(self.parts[1].start)

        def wait(self):
            self.parts[0].wait()
            pl.when(self.more)(self.parts[1].wait)

    def vector_copy(q):
        return pltpu.make_async_copy(
            vectors.at[rows(q * 2 * B, 2 * B), :], vbuf.at[q % VRING], vsem.at[q % VRING]
        )

    def take_vectors(q):
        vector_copy(q).wait()
        at = rows(q * 2 * B, 2 * B)
        vh[at, :], vl[at, :] = split(vbuf[q % VRING])

    for r in range(RING):
        block_copy(r).start()
        if r % 2 and r // 2 < VRING:
            vector_copy(r // 2).start()
    sbuf[RING * SLOTS] = jnp.zeros((B, B), F32)
    first = columns[0, 0]

    def clear(r, _):
        for k in range(16):
            table[r * 16 + k] = DEAD
        return 0

    def fill(r, _):
        fill_table(table, columns, counts, first, r)
        return 0

    lax.fori_loop(0, ROWS + 10, clear, 0)
    lax.fori_loop(0, ROWS, fill, 0)

    def fetch(slot):
        return sbuf[jnp.where(slot < DEAD, slot % (RING * SLOTS), RING * SLOTS)]

    def build(p):
        left, right = window_of(p)
        for h in range(2):
            i = 2 * p + h
            at = slice(h * B, h * B + B)
            for c in range(left // B, right // B):
                o = c - 4 - h
                cols = slice(c * B, c * B + B)
                if abs(o) > REACH:
                    parts = (jnp.zeros((B, B), BF16),) * 2
                else:
                    parts = split(fetch(table[place(i, o)]) + fetch(table[place(i + o, -o)]).T)
                hh[p, at, cols], hl[p, at, cols] = parts

    rows_in = vectors_in = 0
    rows_out, vectors_out = RING, VRING
    before = ()
    for group in GROUPS + ((),):
        if group:
            while rows_out < min(ROWS, RING + 2 * group[0] - REACH):
                block_copy(rows_out).start()
                rows_out += 1
            while rows_in < min(ROWS, 2 * group[-1] + 6):
                block_copy(rows_in).wait()
                rows_in += 1
            while vectors_in < min(PANELS, group[-1] + 3):
                take_vectors(vectors_in)
                vectors_in += 1
            while vectors_out < min(PANELS, VRING + vectors_in):
                vector_copy(vectors_out).start()
                vectors_out += 1
        for k in range(max(len(group), len(before))):
            if k < len(group):
                build(group[k])
            if k < len(before):
                store_rows(before[k], 0.5 * apply_panel(before[k], hh, hl, vh, vl), uh, ul, part)
        before = group


def inner_kernel(hh, hl, vh, vl, ph, pr, uh, ul, part, *gram):
    for p in range(PANELS):
        at = slice(p * 2 * B, (p + 1) * 2 * B)
        prior = ph[at, :].astype(F32) + pr[at, :].astype(F32)
        store_rows(p, apply_panel(p, hh, hl, vh, vl) - prior, uh, ul, part)
    if gram:
        gram[0][0], gram[0][1] = gram_parts(slice(EDGE, LOCAL - EDGE), uh, ul)


def gram_parts(at, high, low):
    over = (((0,), (0,)), ((), ()))
    flipped = high[at, :]
    return (
        lax.dot_general(flipped, high[at, :], over, preferred_element_type=F32),
        lax.dot_general(flipped, low[at, :], over, preferred_element_type=F32),
    )


def cross(xh, xl, side, halo_high, halo_low):
    return dot(xh[side], halo_high) + dot(xl[side], halo_high) + dot(xh[side], halo_low)


def write_edge(side, value, uh, ul):
    start = 0 if side == 0 else LOCAL - EDGE
    uh[start : start + EDGE, :], ul[start : start + EDGE, :] = split(value)


def first_edge_kernel(
    sent_far, sent_near, got_far, got_near, part, uh_in, ul_in, *rest
):
    uh, ul, xh, xl, far, near = rest[KEPT:]
    del uh_in, ul_in
    by_side(
        functools.partial(first_edges, part, uh, ul, xh, xl),
        (sent_far, sent_near),
        (got_far, got_near),
        (far, near),
    )


def by_side(work, *pairs):
    even = even_core()

    @pl.when(even)
    def _():
        work(*pairs)

    @pl.when(jnp.logical_not(even))
    def _():
        work(*((near, far) for far, near in pairs))


def first_edges(part, uh, ul, xh, xl, own, got, out):
    zero = jnp.zeros((B, B), BF16)
    for r in range(REACH):
        for c in range(REACH):
            at, cols = slice(r * B, r * B + B), slice(c * B, c * B + B)
            for side in range(2):
                if (c >= r) if side == 0 else (c <= r):
                    if side == 0:
                        a = PAIRS_PREV.index((r, c - 4 - r)) * B
                        b = PAIRS_NEXT.index((28 + c, 4 + r - c)) * B
                    else:
                        a = PAIRS_NEXT.index((28 + r, 4 + c - r)) * B
                        b = PAIRS_PREV.index((c, r - c - 4)) * B
                    parts = split(own[side][a : a + B, :] + got[side][b : b + B, :].T)
                else:
                    parts = (zero, zero)
                xh[side, at, cols], xl[side, at, cols] = parts
    for side in range(2):
        halves = [
            split(got[side][10 * B + half * EDGE : 10 * B + (half + 1) * EDGE, :]) for half in range(2)
        ]
        high = jnp.concatenate([halves[0][0], halves[1][0]], axis=1)
        low = jnp.concatenate([halves[0][1], halves[1][1]], axis=1)
        value = part[side * EDGE : (side + 1) * EDGE, :] + 0.5 * cross(xh, xl, side, high, low)
        write_edge(side, value, uh, ul)
        out[side][...] = value


def finish_edges(xh, xl, part, uh, ul, got, out=()):
    for side in range(2):
        halo = split(got[side][...])
        value = part[side * EDGE : (side + 1) * EDGE, :] + cross(xh, xl, side, *halo)
        write_edge(side, value, uh, ul)
        if out:
            out[side][...] = value


def edge_kernel(xh, xl, got_far, got_near, part, uh_in, ul_in, *rest):
    uh, ul, far, near = rest[KEPT:]
    del uh_in, ul_in
    work = functools.partial(finish_edges, xh, xl, part, uh, ul)
    by_side(work, (got_far, got_near), (far, near))


def last_edge_kernel(xh, xl, got_far, got_near, part, uh_in, ul_in, inside, uh, ul, mine, theirs):
    del uh_in, ul_in
    even = even_core()
    by_side(functools.partial(finish_edges, xh, xl, part, uh, ul), (got_far, got_near))
    first = gram_parts(slice(0, EDGE), uh, ul)
    last = gram_parts(slice(LOCAL - EDGE, LOCAL), uh, ul)
    main, mixed = (inside[k] + (first[k] + last[k]) for k in range(2))
    total = main + mixed + mixed.T
    r = lax.broadcasted_iota(jnp.int32, (B, B), 0)
    c = lax.broadcasted_iota(jnp.int32, (B, B), 1)
    corner, beside = total[B:, B:], total[:B, B:]
    square = jnp.where(c >= r, total[:B, :B], corner)
    diagonal = jnp.broadcast_to(jnp.sum(jnp.where(r == c, corner, 0.0), axis=0, keepdims=True), (8, B))
    none = jnp.zeros((8, B), F32)
    mine[:B, :] = jnp.where(even, square, beside)
    mine[B:, :] = jnp.where(even, diagonal, none)
    theirs[:B, :] = jnp.where(even, beside, square)
    theirs[B:, :] = jnp.where(even, none, diagonal)


def precise(a, b, over=(((1,), (0,)), ((), ()))):
    return lax.dot_general(
        a, b, over, precision=lax.Precision.HIGHEST, preferred_element_type=F32
    )


def close(a, b, over=(((1,), (0,)), ((), ()))):
    (ah, al), (bh, bl) = split(a), split(b)

    def product(x, y):
        return lax.dot_general(x, y, over, preferred_element_type=F32)

    return product(ah, bh) + (product(ah, bl) + product(al, bh))


def basis_kernel(root, mine, other, uh, ul, basis, factor, work, upper, inverse, out, sems):
    r = lax.broadcasted_iota(jnp.int32, (B, B), 0)
    c = lax.broadcasted_iota(jnp.int32, (B, B), 1)
    even = even_core()
    ad = jnp.where(even, mine[...], other[...])
    b = jnp.where(even, other[:B, :], mine[:B, :])
    square = ad[:B, :]
    high_part = jnp.where(c >= r, square, 0.0)
    low_part = jnp.where(c < r, square, 0.0)
    work[:B, :B] = high_part + jnp.where(c > r, square, 0.0).T
    work[:B, B:] = b
    work[B:, :B] = b.T
    work[B:, B:] = low_part + low_part.T + jnp.where(r == c, ad[B : B + 1, :], 0.0)

    r = lax.broadcasted_iota(jnp.int32, (K, K), 0)
    c = lax.broadcasted_iota(jnp.int32, (K, K), 1)
    gram = work[...]
    eye = jnp.where(r == c, 1.0, 0.0).astype(F32)
    on = jnp.where(r == c, gram, 0.0)
    row_d = jnp.sum(on, axis=0, keepdims=True)
    col_d = jnp.sum(on, axis=1, keepdims=True)
    row_s, col_s = lax.rsqrt(row_d), lax.rsqrt(col_d)
    scaled = gram * row_s * col_s
    work[...] = scaled
    gap = jnp.where(r == c, 0.0, scaled)

    def half_upper(e):
        return jnp.where(c > r, e, jnp.where(c == r, 0.5 * e, 0.0))

    left = (((0,), (0,)), ((), ()))

    def measured(y):
        e = close(y, close(scaled, y), left) - eye
        return jnp.sum(e * e), e, y

    def more(state):
        return (state[0] > 1e-7) & (state[0] < 4.0) & (state[3] < 12)

    def newton(state):
        _, e, y, count = state
        return (*measured(y - close(y, half_upper(e))), count + 1)

    size, _, y, _ = lax.while_loop(more, newton, (*measured(eye - half_upper(gap)), 0))
    settled = (size <= 1e-7) & (jnp.min(jnp.where(r == c, y, 1.0)) > 0.0)

    @pl.when(settled)
    def _():
        inverse[...] = y
        full = close(y, scaled, left)
        upper[...] = jnp.where(c >= r, full, 0.0)

    @pl.when(jnp.logical_not(settled))
    def _():
        lane = lax.broadcasted_iota(jnp.int32, (1, K), 1)
        down = lax.broadcasted_iota(jnp.int32, (K, 1), 0)

        def column(k, _):
            a = work[...]
            row = work[pl.ds(k, 1), :]
            root = lax.rsqrt(jnp.sum(jnp.where(lane == k, row, 0.0)))
            row = jnp.where(lane >= k, row * root, 0.0)
            col = jnp.sum(jnp.where(c == k, a, 0.0), axis=1, keepdims=True)
            col = jnp.where(down >= k, col * root, 0.0)
            upper[pl.ds(k, 1), :] = row
            work[...] = a - col * row
            return 0

        lax.fori_loop(0, K, column, 0)
        inverse[...] = jnp.zeros((K, K), F32)

        def back(t, _):
            k = K - 1 - t
            row = upper[pl.ds(k, 1), :]
            pivot = jnp.sum(jnp.where(lane == k, row, 0.0))
            rest = jnp.broadcast_to(jnp.where(lane > k, row, 0.0), (8, K))
            known = precise(rest, inverse[...])[:1, :]
            inverse[pl.ds(k, 1), :] = (jnp.where(lane == k, 1.0, 0.0) - known) / pivot
            return 0

        lax.fori_loop(0, K, back, 0)

    factor[...] = upper[...] * (row_d * row_s) / root
    wh, wl = split(inverse[...] * (col_s * root))

    def out_copy(q):
        at = rows(q * CHUNK, CHUNK)
        return pltpu.make_async_copy(out.at[at, :], basis.at[at, :], sems.at[q])

    def step(q, _):
        at = rows(q * CHUNK, CHUNK)
        out[at, :] = dot(uh[at, :], wh) + dot(ul[at, :], wh) + dot(uh[at, :], wl)
        out_copy(q).start()
        return 0

    lax.fori_loop(0, LOCAL // CHUNK, step, 0)
    for q in range(LOCAL // CHUNK):
        out_copy(q).wait()


def swap_pairs(far, near):
    count = lax.axis_size(ALL)
    pairs = [(i, i + 1) for i in range(1, count - 1, 2)]
    got_far = lax.ppermute(far, ALL, pairs + [(j, i) for i, j in pairs])
    got_near = lax.ppermute(near, "c", [(0, 1), (1, 0)])
    return got_far, got_near


def group_sum(value, axis):
    count = lax.axis_size(axis)
    one, two, three = (
        lax.ppermute(value, axis, [(i, i ^ k) for i in range(count)]) for k in (1, 2, 3)
    )
    return (value + one) + (two + three)


def body(blocks, columns, counts, start_vectors):
    flat, start_vectors, counts, columns = (
        pltpu.with_memory_space_constraint(x, pltpu.HBM)
        for x in (blocks.reshape(DEAD, B, B), start_vectors, counts, columns.T)
    )
    packed = pltpu.VMEM((PACKED, B), F32)
    sent = pl.pallas_call(
        pack_kernel,
        out_shape=(packed, packed),
        in_specs=(SM, SM, HB, HB),
        out_specs=(VM, VM),
        scratch_shapes=[
            pltpu.SMEM((TABLE + 1,), jnp.int32),
            pltpu.VMEM((B, B), F32),
            pltpu.SemaphoreType.DMA((24,)),
        ],
        compiler_params=params(2),
        cost_estimate=cost(0, 2 * 2 * PACKED * B * 4),
        name="pack_edges",
    )(columns, counts, flat, start_vectors)
    got = swap_pairs(*sent)

    wide = pltpu.VMEM((PANELS, 2 * B, WIDE), BF16)
    slab = pltpu.VMEM((LOCAL, K), BF16)
    partial = pltpu.VMEM((2 * EDGE, K), F32)
    crossing = pltpu.VMEM((2, EDGE, EDGE), BF16)
    edge = jax.ShapeDtypeStruct((EDGE, K), F32)
    flops = 3 * 2 * PANELS * 2 * B * WIDE * K
    hh, hl, vh, vl, uh, ul, part = pl.pallas_call(
        first_kernel,
        out_shape=(wide, wide, slab, slab, slab, slab, partial),
        in_specs=(SM, SM, HB, HB),
        out_specs=(VM,) * 7,
        scratch_shapes=[
            pltpu.SMEM((TABLE + 1,), jnp.int32),
            pltpu.VMEM((RING * SLOTS + 1, B, B), F32),
            pltpu.VMEM((VRING, 2 * B, K), F32),
        ]
        + [pltpu.SemaphoreType.DMA((RING, 2)), pltpu.SemaphoreType.DMA((VRING,))],
        compiler_params=params(16),
        cost_estimate=cost(flops * 2, 24 * 2**20),
        name="first_inner",
    )(columns, counts, flat, start_vectors)

    uh, ul, xh, xl, far, near = pl.pallas_call(
        first_edge_kernel,
        out_shape=(slab, slab, crossing, crossing, edge, edge),
        in_specs=(VM,) * (7 + KEPT),
        out_specs=(VM,) * 6,
        input_output_aliases={5: 0, 6: 1},
        compiler_params=params(4),
        cost_estimate=cost(8e8, 6 * 2**20),
        name="first_edge",
    )(*sent, *got, part, uh, ul, hh, hl, vh, vl)

    def inner(vectors, prior, *gram):
        return pl.pallas_call(
            inner_kernel,
            out_shape=(slab, slab, partial) + gram,
            in_specs=(VM,) * 6,
            out_specs=(VM,) * (3 + len(gram)),
            compiler_params=params(6),
            cost_estimate=cost(flops, 2**20),
            name="inner",
        )(hh, hl, *vectors, *prior)

    got = swap_pairs(far, near)
    wh, wl, part = inner((uh, ul), (vh, vl))
    wh, wl, far, near = pl.pallas_call(
        edge_kernel,
        out_shape=(slab, slab, edge, edge),
        in_specs=(VM,) * (7 + KEPT),
        out_specs=(VM,) * 4,
        input_output_aliases={5: 0, 6: 1},
        compiler_params=params(8),
        cost_estimate=cost(8e8, 2 * 2**20),
        name="edge",
    )(xh, xl, *got, part, wh, wl, hh, hl, uh, ul)

    got = swap_pairs(far, near)
    fh, fl, part, inside = inner((wh, wl), (uh, ul), pltpu.VMEM((2, K, K), F32))
    half = pltpu.VMEM((B + 8, B), F32)
    fh, fl, mine, theirs = pl.pallas_call(
        last_edge_kernel,
        out_shape=(slab, slab, half, half),
        in_specs=(VM,) * 8,
        out_specs=(VM,) * 4,
        input_output_aliases={5: 0, 6: 1},
        compiler_params=params(8),
        cost_estimate=cost(2e9, 2 * 2**20),
        name="last_edge_gram",
    )(xh, xl, *got, part, fh, fl, inside)

    swap = [(0, 1), (1, 0)]
    mine = mine + lax.ppermute(theirs, "c", swap)
    for axis in ("y", "x", "z"):
        mine = group_sum(mine, axis)
    other = lax.ppermute(mine, "c", swap)

    total_rows = LOCAL * lax.axis_size(ALL)
    basis, factor = pl.pallas_call(
        functools.partial(basis_kernel, math.sqrt(total_rows)),
        out_shape=(jax.ShapeDtypeStruct((LOCAL, K), F32), jax.ShapeDtypeStruct((K, K), F32)),
        in_specs=(VM,) * 4,
        out_specs=(HB, VM),
        scratch_shapes=[pltpu.VMEM((K, K), F32)] * 3
        + [pltpu.VMEM((LOCAL, K), F32), pltpu.SemaphoreType.DMA((LOCAL // CHUNK,))],
        compiler_params=params(12),
        cost_estimate=cost(2e9, 4 * 2**20),
        name="basis",
    )(mine, other, fh, fl)
    return basis, factor


def solution(mesh):
    fine = Mesh(mesh.devices.reshape(4, 4, 4, 2), ALL)
    placed = (P(ALL, None, None, None), P(ALL, None), P(ALL), P(ALL, None))
    return jax.shard_map(
        body, mesh=fine, in_specs=placed, out_specs=(P(ALL, None), P()), check_vma=False
    )
```

```python
import functools
import math

import jax
import jax.numpy as jnp
from jax import lax
from jax.experimental import pallas as pl
from jax.experimental.pallas import tpu as pltpu
from jax.sharding import Mesh, PartitionSpec as P

B = 128
K = 256
ROWS = 32
SLOTS = 8
REACH = 4
PANELS = ROWS // 2
WIDE = 10 * B
EDGE = REACH * B
LOCAL = ROWS * B
DEAD = ROWS * SLOTS
TABLE = (ROWS + 10) * 16
RING = 24
VRING = 8
GROUPS = ((0, 1), (2, 3, 4, 5), (6, 7, 8, 9), (10, 11, 12, 13), (14, 15))
KEPT = 4
CHUNK = 2048
PAIRS_PREV = [(r, o) for r in range(4) for o in range(-4, 0) if r + o < 0]
PAIRS_NEXT = [(r, o) for r in range(28, 32) for o in range(1, 5) if r + o > 31]
PACKED = 10 * B + 2 * EDGE

F32 = jnp.float32
BF16 = jnp.bfloat16
VM = pl.BlockSpec(memory_space=pltpu.VMEM)
SM = pl.BlockSpec(memory_space=pltpu.SMEM)
HB = pl.BlockSpec(memory_space=pltpu.HBM)
ALL = ("y", "x", "z", "c")


def params(mib):
    return pltpu.CompilerParams(vmem_limit_bytes=mib * 2**20)


def cost(flops, moved):
    return pl.CostEstimate(flops=int(flops), bytes_accessed=int(moved), transcendentals=0)


def dot(a, b):
    return jnp.dot(a, b, preferred_element_type=F32)


def split(x):
    high = x.astype(BF16)
    return high, (x - high.astype(F32)).astype(BF16)


def rows(start, size):
    return pl.ds(pl.multiple_of(start, size), size)


def place(r, o):
    return (r + 5) * 16 + o + 5


def fill_table(table, columns, counts, first, r):
    for s in range(SLOTS):
        offset = columns[s, r] - first - r
        table[jnp.where(s < counts[r], place(r, offset), TABLE)] = r * SLOTS + s


def clear_table(table, start, stop):
    for k in range(start, stop):
        table[k] = DEAD


def even_core():
    return lax.axis_index("c") == 0


def scalar_copies(columns_in, counts_in, columns, counts, sems):
    return (
        pltpu.make_async_copy(columns_in, columns, sems.at[0]),
        pltpu.make_async_copy(counts_in, counts, sems.at[1]),
    )


def pack_kernel(
    columns_in, counts_in, blocks, vectors, swap_far, swap_near, columns, counts, table, zero, sems, scalar_sems
):
    scalars = scalar_copies(columns_in, counts_in, columns, counts, scalar_sems)
    for copy in scalars:
        copy.start()

    def vector_moves(to_prev, to_next):
        return [
            pltpu.make_async_copy(
                vectors.at[pl.ds(start, EDGE), pl.ds(half * B, B)],
                out.at[pl.ds(10 * B + half * EDGE, EDGE), :],
                sems.at[side * 12 + 10 + half],
            )
            for side, (out, start) in enumerate(((to_prev, 0), (to_next, LOCAL - EDGE)))
            for half in range(2)
        ]

    def begin(pair):
        for move in vector_moves(*pair):
            move.start()

    by_side(begin, (swap_far, swap_near))
    zero[...] = jnp.zeros_like(zero)
    for r in (0, 1, 2, 3, 28, 29, 30, 31):
        clear_table(table, place(r, -4), place(r, 5))
    for copy in scalars:
        copy.wait()
    first = columns[0, 0]
    for r in (0, 1, 2, 3, 28, 29, 30, 31):
        fill_table(table, columns, counts, first, r)

    def fill(pair):
        moves = vector_moves(*pair)
        for side, (out, pairs) in enumerate(zip(pair, (PAIRS_PREV, PAIRS_NEXT))):
            for k, (r, o) in enumerate(pairs):
                slot = table[place(r, o)]
                target = out.at[pl.ds(k * B, B), :]
                sem = sems.at[side * 12 + k]

                @pl.when(slot < DEAD)
                def _():
                    pltpu.make_async_copy(blocks.at[slot], target, sem).start()

                @pl.when(slot >= DEAD)
                def _():
                    pltpu.make_async_copy(zero, target, sem).start()

                moves.append(pltpu.make_async_copy(zero, target, sem))
        for move in moves:
            move.wait()

    by_side(fill, (swap_far, swap_near))


def window_of(p):
    return max(0, (2 - p) * 2 * B), WIDE - max(0, (p - PANELS + 3) * 2 * B)


def apply_panel(p, hh, hl, vh, vl):
    left, right = window_of(p)
    window = slice(p * 2 * B + left - EDGE, p * 2 * B + right - EDGE)
    high, low = hh[p, :, left:right], hl[p, :, left:right]
    return dot(high, vh[window, :]) + dot(low, vh[window, :]) + dot(high, vl[window, :])


def store_rows(p, value, uh, ul, part):
    at = slice(p * 2 * B, (p + 1) * 2 * B)
    uh[at, :], ul[at, :] = split(value)
    if p < 2:
        part[p * 2 * B : (p + 1) * 2 * B, :] = value
    elif p >= PANELS - 2:
        part[(p - PANELS + 4) * 2 * B : (p - PANELS + 5) * 2 * B, :] = value


def first_kernel(
    columns_in, counts_in, blocks, vectors, hh, hl, vh, vl, uh, ul, part,
    columns, counts, table, sbuf, vbuf, ssem, vsem, scalar_sems,
):
    class block_copy:
        def __init__(self, r):
            self.row = r

        def part(self, k):
            r = self.row
            return pltpu.make_async_copy(
                blocks.at[pl.ds(r * SLOTS + k * 4, SLOTS // 2)],
                sbuf.at[pl.ds((r % RING) * SLOTS + k * 4, SLOTS // 2)],
                ssem.at[r % RING, k],
            )

        def start(self):
            self.part(0).start()
            self.start_more()

        def start_more(self):
            pl.when(counts[self.row] > SLOTS // 2)(lambda: self.part(1).start())

        def wait(self):
            self.part(0).wait()
            pl.when(counts[self.row] > SLOTS // 2)(lambda: self.part(1).wait())

    def vector_copy(q):
        return pltpu.make_async_copy(
            vectors.at[rows(q * 2 * B, 2 * B), :], vbuf.at[q % VRING], vsem.at[q % VRING]
        )

    def take_vectors(q):
        vector_copy(q).wait()
        at = rows(q * 2 * B, 2 * B)
        vh[at, :], vl[at, :] = split(vbuf[q % VRING])

    scalars = scalar_copies(columns_in, counts_in, columns, counts, scalar_sems)
    for copy in scalars:
        copy.start()
    for r in range(RING):
        block_copy(r).part(0).start()
        if r % 2 and r // 2 < VRING:
            vector_copy(r // 2).start()
    sbuf[RING * SLOTS] = jnp.zeros((B, B), F32)
    for copy in scalars:
        copy.wait()
    for r in range(RING):
        block_copy(r).start_more()
    first = columns[0, 0]

    def clear(r, _):
        for k in range(16):
            table[r * 16 + k] = DEAD
        return 0

    def fill(r, _):
        fill_table(table, columns, counts, first, r)
        return 0

    lax.fori_loop(0, ROWS + 10, clear, 0)
    lax.fori_loop(0, ROWS, fill, 0)

    def fetch(slot):
        return sbuf[jnp.where(slot < DEAD, slot % (RING * SLOTS), RING * SLOTS)]

    def build(p):
        left, right = window_of(p)
        for h in range(2):
            i = 2 * p + h
            at = slice(h * B, h * B + B)
            for c in range(left // B, right // B):
                o = c - 4 - h
                cols = slice(c * B, c * B + B)
                if abs(o) > REACH:
                    parts = (jnp.zeros((B, B), BF16),) * 2
                else:
                    parts = split(fetch(table[place(i, o)]) + fetch(table[place(i + o, -o)]).T)
                hh[p, at, cols], hl[p, at, cols] = parts

    rows_in = vectors_in = 0
    rows_out, vectors_out = RING, VRING
    before = ()
    for group in GROUPS + ((),):
        if group:
            while rows_out < min(ROWS, RING + 2 * group[0] - REACH):
                block_copy(rows_out).start()
                rows_out += 1
            while rows_in < min(ROWS, 2 * group[-1] + 6):
                block_copy(rows_in).wait()
                rows_in += 1
            while vectors_in < min(PANELS, group[-1] + 3):
                take_vectors(vectors_in)
                vectors_in += 1
            while vectors_out < min(PANELS, VRING + vectors_in):
                vector_copy(vectors_out).start()
                vectors_out += 1
        for k in range(max(len(group), len(before))):
            if k < len(group):
                build(group[k])
            if k < len(before):
                store_rows(before[k], 0.5 * apply_panel(before[k], hh, hl, vh, vl), uh, ul, part)
        before = group


def inner_kernel(hh, hl, vh, vl, ph, pr, uh, ul, part, *gram):
    for p in range(PANELS):
        at = slice(p * 2 * B, (p + 1) * 2 * B)
        prior = ph[at, :].astype(F32) + pr[at, :].astype(F32)
        store_rows(p, apply_panel(p, hh, hl, vh, vl) - prior, uh, ul, part)
    if gram:
        gram[0][0], gram[0][1] = gram_parts(slice(EDGE, LOCAL - EDGE), uh, ul)


def gram_parts(at, high, low):
    over = (((0,), (0,)), ((), ()))
    flipped = high[at, :]
    return (
        lax.dot_general(flipped, high[at, :], over, preferred_element_type=F32),
        lax.dot_general(flipped, low[at, :], over, preferred_element_type=F32),
    )


def cross(xh, xl, side, halo_high, halo_low):
    return dot(xh[side], halo_high) + dot(xl[side], halo_high) + dot(xh[side], halo_low)


def write_edge(side, value, uh, ul):
    start = 0 if side == 0 else LOCAL - EDGE
    uh[start : start + EDGE, :], ul[start : start + EDGE, :] = split(value)


def first_edge_kernel(
    sent_far, sent_near, got_far, got_near, part, uh_in, ul_in, *rest
):
    uh, ul, xh, xl, far, near = rest[KEPT:]
    del uh_in, ul_in
    by_side(
        functools.partial(first_edges, part, uh, ul, xh, xl),
        (sent_far, sent_near),
        (got_far, got_near),
        (far, near),
    )


def by_side(work, *pairs):
    even = even_core()

    @pl.when(even)
    def _():
        work(*pairs)

    @pl.when(jnp.logical_not(even))
    def _():
        work(*((near, far) for far, near in pairs))


def first_edges(part, uh, ul, xh, xl, own, got, out):
    zero = jnp.zeros((B, B), BF16)
    for r in range(REACH):
        for c in range(REACH):
            at, cols = slice(r * B, r * B + B), slice(c * B, c * B + B)
            for side in range(2):
                if (c >= r) if side == 0 else (c <= r):
                    if side == 0:
                        a = PAIRS_PREV.index((r, c - 4 - r)) * B
                        b = PAIRS_NEXT.index((28 + c, 4 + r - c)) * B
                    else:
                        a = PAIRS_NEXT.index((28 + r, 4 + c - r)) * B
                        b = PAIRS_PREV.index((c, r - c - 4)) * B
                    parts = split(own[side][a : a + B, :] + got[side][b : b + B, :].T)
                else:
                    parts = (zero, zero)
                xh[side, at, cols], xl[side, at, cols] = parts
    for side in range(2):
        halves = [
            split(got[side][10 * B + half * EDGE : 10 * B + (half + 1) * EDGE, :]) for half in range(2)
        ]
        high = jnp.concatenate([halves[0][0], halves[1][0]], axis=1)
        low = jnp.concatenate([halves[0][1], halves[1][1]], axis=1)
        value = part[side * EDGE : (side + 1) * EDGE, :] + 0.5 * cross(xh, xl, side, high, low)
        write_edge(side, value, uh, ul)
        out[side][...] = value


def finish_edges(xh, xl, part, uh, ul, got, out=()):
    for side in range(2):
        halo = split(got[side][...])
        value = part[side * EDGE : (side + 1) * EDGE, :] + cross(xh, xl, side, *halo)
        write_edge(side, value, uh, ul)
        if out:
            out[side][...] = value


def edge_kernel(xh, xl, got_far, got_near, part, uh_in, ul_in, *rest):
    uh, ul, far, near = rest[KEPT:]
    del uh_in, ul_in
    work = functools.partial(finish_edges, xh, xl, part, uh, ul)
    by_side(work, (got_far, got_near), (far, near))


def last_edge_kernel(xh, xl, got_far, got_near, part, uh_in, ul_in, inside, uh, ul, mine, theirs):
    del uh_in, ul_in
    even = even_core()
    by_side(functools.partial(finish_edges, xh, xl, part, uh, ul), (got_far, got_near))
    first = gram_parts(slice(0, EDGE), uh, ul)
    last = gram_parts(slice(LOCAL - EDGE, LOCAL), uh, ul)
    main, mixed = (inside[k] + (first[k] + last[k]) for k in range(2))
    total = main + mixed + mixed.T
    r = lax.broadcasted_iota(jnp.int32, (B, B), 0)
    c = lax.broadcasted_iota(jnp.int32, (B, B), 1)
    corner, beside = total[B:, B:], total[:B, B:]
    square = jnp.where(c >= r, total[:B, :B], corner)
    diagonal = jnp.broadcast_to(jnp.sum(jnp.where(r == c, corner, 0.0), axis=0, keepdims=True), (8, B))
    none = jnp.zeros((8, B), F32)
    mine[:B, :] = jnp.where(even, square, beside)
    mine[B:, :] = jnp.where(even, diagonal, none)
    theirs[:B, :] = jnp.where(even, beside, square)
    theirs[B:, :] = jnp.where(even, none, diagonal)


def precise(a, b, over=(((1,), (0,)), ((), ()))):
    return lax.dot_general(
        a, b, over, precision=lax.Precision.HIGHEST, preferred_element_type=F32
    )


def close(a, b, over=(((1,), (0,)), ((), ()))):
    (ah, al), (bh, bl) = split(a), split(b)

    def product(x, y):
        return lax.dot_general(x, y, over, preferred_element_type=F32)

    return product(ah, bh) + (product(ah, bl) + product(al, bh))


def basis_kernel(root, mine, other, uh, ul, basis, factor, work, upper, inverse, out, sems):
    r = lax.broadcasted_iota(jnp.int32, (B, B), 0)
    c = lax.broadcasted_iota(jnp.int32, (B, B), 1)
    even = even_core()
    ad = jnp.where(even, mine[...], other[...])
    b = jnp.where(even, other[:B, :], mine[:B, :])
    square = ad[:B, :]
    high_part = jnp.where(c >= r, square, 0.0)
    low_part = jnp.where(c < r, square, 0.0)
    work[:B, :B] = high_part + jnp.where(c > r, square, 0.0).T
    work[:B, B:] = b
    work[B:, :B] = b.T
    work[B:, B:] = low_part + low_part.T + jnp.where(r == c, ad[B : B + 1, :], 0.0)

    r = lax.broadcasted_iota(jnp.int32, (K, K), 0)
    c = lax.broadcasted_iota(jnp.int32, (K, K), 1)
    gram = work[...]
    eye = jnp.where(r == c, 1.0, 0.0).astype(F32)
    on = jnp.where(r == c, gram, 0.0)
    row_d = jnp.sum(on, axis=0, keepdims=True)
    col_d = jnp.sum(on, axis=1, keepdims=True)
    row_s, col_s = lax.rsqrt(row_d), lax.rsqrt(col_d)
    scaled = gram * row_s * col_s
    work[...] = scaled
    gap = jnp.where(r == c, 0.0, scaled)

    def half_upper(e):
        return jnp.where(c > r, e, jnp.where(c == r, 0.5 * e, 0.0))

    left = (((0,), (0,)), ((), ()))

    def measured(y):
        e = close(y, close(scaled, y), left) - eye
        return jnp.sum(e * e), e, y

    def more(state):
        return (state[0] > 1e-7) & (state[0] < 4.0) & (state[3] < 12)

    def newton(state):
        _, e, y, count = state
        return (*measured(y - close(y, half_upper(e))), count + 1)

    size, _, y, _ = lax.while_loop(more, newton, (*measured(eye - half_upper(gap)), 0))
    settled = (size <= 1e-7) & (jnp.min(jnp.where(r == c, y, 1.0)) > 0.0)

    @pl.when(settled)
    def _():
        inverse[...] = y
        full = close(y, scaled, left)
        upper[...] = jnp.where(c >= r, full, 0.0)

    @pl.when(jnp.logical_not(settled))
    def _():
        lane = lax.broadcasted_iota(jnp.int32, (1, K), 1)
        down = lax.broadcasted_iota(jnp.int32, (K, 1), 0)

        def column(k, _):
            a = work[...]
            row = work[pl.ds(k, 1), :]
            root = lax.rsqrt(jnp.sum(jnp.where(lane == k, row, 0.0)))
            row = jnp.where(lane >= k, row * root, 0.0)
            col = jnp.sum(jnp.where(c == k, a, 0.0), axis=1, keepdims=True)
            col = jnp.where(down >= k, col * root, 0.0)
            upper[pl.ds(k, 1), :] = row
            work[...] = a - col * row
            return 0

        lax.fori_loop(0, K, column, 0)
        inverse[...] = jnp.zeros((K, K), F32)

        def back(t, _):
            k = K - 1 - t
            row = upper[pl.ds(k, 1), :]
            pivot = jnp.sum(jnp.where(lane == k, row, 0.0))
            rest = jnp.broadcast_to(jnp.where(lane > k, row, 0.0), (8, K))
            known = precise(rest, inverse[...])[:1, :]
            inverse[pl.ds(k, 1), :] = (jnp.where(lane == k, 1.0, 0.0) - known) / pivot
            return 0

        lax.fori_loop(0, K, back, 0)

    factor[...] = upper[...] * (row_d * row_s) / root
    wh, wl = split(inverse[...] * (col_s * root))

    def out_copy(q):
        at = rows(q * CHUNK, CHUNK)
        return pltpu.make_async_copy(out.at[at, :], basis.at[at, :], sems.at[q])

    def step(q, _):
        at = rows(q * CHUNK, CHUNK)
        out[at, :] = dot(uh[at, :], wh) + dot(ul[at, :], wh) + dot(uh[at, :], wl)
        out_copy(q).start()
        return 0

    lax.fori_loop(0, LOCAL // CHUNK, step, 0)
    for q in range(LOCAL // CHUNK):
        out_copy(q).wait()


def swap_pairs(far, near):
    count = lax.axis_size(ALL)
    pairs = [(i, i + 1) for i in range(1, count - 1, 2)]
    got_far = lax.ppermute(far, ALL, pairs + [(j, i) for i, j in pairs])
    got_near = lax.ppermute(near, "c", [(0, 1), (1, 0)])
    return got_far, got_near


def group_sum(value, axis):
    count = lax.axis_size(axis)
    one, two, three = (
        lax.ppermute(value, axis, [(i, i ^ k) for i in range(count)]) for k in (1, 2, 3)
    )
    return (value + one) + (two + three)


def body(blocks, columns, counts, start_vectors):
    flat, start_vectors, counts, columns = (
        pltpu.with_memory_space_constraint(x, pltpu.HBM)
        for x in (blocks.reshape(DEAD, B, B), start_vectors, counts, columns.T)
    )
    packed = pltpu.VMEM((PACKED, B), F32)
    sent = pl.pallas_call(
        pack_kernel,
        out_shape=(packed, packed),
        in_specs=(HB,) * 4,
        out_specs=(VM, VM),
        scratch_shapes=[
            pltpu.SMEM((SLOTS, ROWS), jnp.int32),
            pltpu.SMEM((ROWS,), jnp.int32),
            pltpu.SMEM((TABLE + 1,), jnp.int32),
            pltpu.VMEM((B, B), F32),
            pltpu.SemaphoreType.DMA((24,)),
            pltpu.SemaphoreType.DMA((2,)),
        ],
        compiler_params=params(2),
        cost_estimate=cost(0, 2 * 2 * PACKED * B * 4),
        name="pack_edges",
    )(columns, counts, flat, start_vectors)
    got = swap_pairs(*sent)

    wide = pltpu.VMEM((PANELS, 2 * B, WIDE), BF16)
    slab = pltpu.VMEM((LOCAL, K), BF16)
    partial = pltpu.VMEM((2 * EDGE, K), F32)
    crossing = pltpu.VMEM((2, EDGE, EDGE), BF16)
    edge = jax.ShapeDtypeStruct((EDGE, K), F32)
    flops = 3 * 2 * PANELS * 2 * B * WIDE * K
    hh, hl, vh, vl, uh, ul, part = pl.pallas_call(
        first_kernel,
        out_shape=(wide, wide, slab, slab, slab, slab, partial),
        in_specs=(HB,) * 4,
        out_specs=(VM,) * 7,
        scratch_shapes=[
            pltpu.SMEM((SLOTS, ROWS), jnp.int32),
            pltpu.SMEM((ROWS,), jnp.int32),
            pltpu.SMEM((TABLE + 1,), jnp.int32),
            pltpu.VMEM((RING * SLOTS + 1, B, B), F32),
            pltpu.VMEM((VRING, 2 * B, K), F32),
        ]
        + [pltpu.SemaphoreType.DMA((RING, 2)), pltpu.SemaphoreType.DMA((VRING,))]
        + [pltpu.SemaphoreType.DMA((2,))],
        compiler_params=params(16),
        cost_estimate=cost(flops * 2, 24 * 2**20),
        name="first_inner",
    )(columns, counts, flat, start_vectors)

    uh, ul, xh, xl, far, near = pl.pallas_call(
        first_edge_kernel,
        out_shape=(slab, slab, crossing, crossing, edge, edge),
        in_specs=(VM,) * (7 + KEPT),
        out_specs=(VM,) * 6,
        input_output_aliases={5: 0, 6: 1},
        compiler_params=params(4),
        cost_estimate=cost(8e8, 6 * 2**20),
        name="first_edge",
    )(*sent, *got, part, uh, ul, hh, hl, vh, vl)

    def inner(vectors, prior, *gram):
        return pl.pallas_call(
            inner_kernel,
            out_shape=(slab, slab, partial) + gram,
            in_specs=(VM,) * 6,
            out_specs=(VM,) * (3 + len(gram)),
            compiler_params=params(6),
            cost_estimate=cost(flops, 2**20),
            name="inner",
        )(hh, hl, *vectors, *prior)

    got = swap_pairs(far, near)
    wh, wl, part = inner((uh, ul), (vh, vl))
    wh, wl, far, near = pl.pallas_call(
        edge_kernel,
        out_shape=(slab, slab, edge, edge),
        in_specs=(VM,) * (7 + KEPT),
        out_specs=(VM,) * 4,
        input_output_aliases={5: 0, 6: 1},
        compiler_params=params(8),
        cost_estimate=cost(8e8, 2 * 2**20),
        name="edge",
    )(xh, xl, *got, part, wh, wl, hh, hl, uh, ul)

    got = swap_pairs(far, near)
    fh, fl, part, inside = inner((wh, wl), (uh, ul), pltpu.VMEM((2, K, K), F32))
    half = pltpu.VMEM((B + 8, B), F32)
    fh, fl, mine, theirs = pl.pallas_call(
        last_edge_kernel,
        out_shape=(slab, slab, half, half),
        in_specs=(VM,) * 8,
        out_specs=(VM,) * 4,
        input_output_aliases={5: 0, 6: 1},
        compiler_params=params(8),
        cost_estimate=cost(2e9, 2 * 2**20),
        name="last_edge_gram",
    )(xh, xl, *got, part, fh, fl, inside)

    swap = [(0, 1), (1, 0)]
    mine = mine + lax.ppermute(theirs, "c", swap)
    for axis in ("y", "x", "z"):
        mine = group_sum(mine, axis)
    other = lax.ppermute(mine, "c", swap)

    total_rows = LOCAL * lax.axis_size(ALL)
    basis, factor = pl.pallas_call(
        functools.partial(basis_kernel, math.sqrt(total_rows)),
        out_shape=(jax.ShapeDtypeStruct((LOCAL, K), F32), jax.ShapeDtypeStruct((K, K), F32)),
        in_specs=(VM,) * 4,
        out_specs=(HB, VM),
        scratch_shapes=[pltpu.VMEM((K, K), F32)] * 3
        + [pltpu.VMEM((LOCAL, K), F32), pltpu.SemaphoreType.DMA((LOCAL // CHUNK,))],
        compiler_params=params(12),
        cost_estimate=cost(2e9, 4 * 2**20),
        name="basis",
    )(mine, other, fh, fl)
    return basis, factor


def solution(mesh):
    fine = Mesh(mesh.devices.reshape(4, 4, 4, 2), ALL)
    placed = (P(ALL, None, None, None), P(ALL, None), P(ALL), P(ALL, None))
    return jax.shard_map(
        body, mesh=fine, in_specs=placed, out_specs=(P(ALL, None), P()), check_vma=False
    )
```
